32 devices in a mesh: tab: 4 (over x, core), rep: 8 (over z, y).
Axes of the slice: x: 2, y: 2, z: 4, core: 2. Of those that a mesh axis runs over, the one named last changes fastest.
Arguments:
- d_proj: bfloat16 [8, 512, 4, 256], P('rep', 'tab'), may hold values from -6 to 6
- pooled: bfloat16 [8, 512, 4, 512], P('rep', 'tab'), may hold values from -6 to 6
- proj: bfloat16 [4, 512, 256], replicated, may hold values from -0.25 to 0.25
- bag_rows: int32 [8, 512, 4, 8], P('rep', None, 'tab'), may hold values from 0 to 511
- bag_lengths: int32 [8, 512, 4], P('rep', None, 'tab'), may hold values from 1 to 8
- dim_blocks: int32 [4], replicated, may hold values from 1 to 16
Outputs:
- emb_grad: float32 [4, 512, 512], P('tab')
- proj_grad: float32 [4, 512, 256], P('tab')
The draws below stay inside these ranges and needn't reach their ends.
All inputs are finite; a program needn't handle non-finite values.
Results may differ from the reference program's by a relative error of at most 0.003.
Values may be sent and summed in bfloat16 or wider, within the bound.
A program may use at most 64 MiB of HBM per device.

```python
import math
import jax
import jax.numpy as jnp
import numpy as np
from jax import lax

ROWS = 512
BAG = 8
EMAX = 512
P_SIZE = 256
UNIT = 32
TABLES = 4
GROUPS = 8
GROUP_B = 512


def plant(values, key, least, high):
    index_at = [jax.random.randint(jax.random.fold_in(key, axis), (), 0, length) for axis, length in enumerate(values.shape)]
    longest = values.shape.index(max(values.shape))
    neighbour = index_at[:longest] + [(index_at[longest] + 1) % values.shape[longest]] + index_at[longest + 1:]
    return values.at[tuple(index_at)].set(least).at[tuple(neighbour)].set(high)


def block_scale(rng, extent, shards, smallest, top_value):
    factor_of = 1.0
    for position, blocks in shards:
        steps = jax.random.uniform(jax.random.fold_in(jax.random.fold_in(rng, 6), position), (blocks,), jnp.float32, smallest / len(shards), top_value / len(shards))
        factor_of = factor_of * jnp.repeat(jnp.exp(steps), extent[position] // blocks).reshape((-1,) + (1,) * (len(extent) - 1 - position))
    return factor_of


def cumulative_ranks(number_of, skew):
    loads = [(1 << 20) // math.isqrt(standing ** skew) + 1 for standing in range(1, number_of + 1)]
    scale = 1 + sum(loads) // (1 << 30)
    return np.cumsum(np.array([max(1, weight // scale) for weight in loads]))


def ranked(rng, dims, count, skew):
    grid = cumulative_ranks(count, skew)
    pick = jax.random.randint(jax.random.fold_in(rng, 1), dims, 0, int(grid[count - 1]))
    grade = jnp.searchsorted(jnp.asarray(grid, jnp.int32), pick, side="right")
    return jax.random.permutation(jax.random.fold_in(rng, 2), count)[grade].astype(jnp.int32)


def centred(stream_key, dims, scale, reach, shards=(), kind=jnp.bfloat16):
    loudness = block_scale(stream_key, dims, shards, -0.22, 0.18) if shards else 1.0
    drawn = jax.random.normal(stream_key, dims, jnp.float32) * scale * loudness
    return jnp.minimum(jnp.maximum(drawn, -reach), reach).astype(kind)


def setup_inputs(seed: int = 0) -> dict:
    keys = jax.random.split(jax.random.key(seed), 7)
    return {
        "d_proj": centred(keys[0], (GROUPS, GROUP_B, TABLES, P_SIZE), 1.0, 6.0, ((0, 8), (1, 4))),
        "pooled": centred(keys[1], (GROUPS, GROUP_B, TABLES, EMAX), 1.0, 6.0, ((0, 8), (1, 4))),
        "proj": centred(keys[2], (TABLES, EMAX, P_SIZE), EMAX ** -0.5, 0.25),
        "bag_rows": plant(ranked(keys[3], (GROUPS, GROUP_B, TABLES, BAG), ROWS, 2), jax.random.fold_in(keys[3], 3), 0, ROWS - 1).astype(jnp.int32),
        "bag_lengths": plant(jax.random.randint(keys[4], (GROUPS, GROUP_B, TABLES), 1, BAG + 1), jax.random.fold_in(keys[4], 1), 1, BAG).astype(jnp.int32),
        "dim_blocks": plant(jax.random.randint(keys[5], (TABLES,), 1, 17), jax.random.fold_in(keys[5], 1), 1, 16).astype(jnp.int32),
    }


def reference(d_proj, pooled, proj, bag_rows, bag_lengths, dim_blocks):
    columns = jnp.arange(EMAX, dtype=jnp.int32)
    live = (columns[None, :] < (UNIT * dim_blocks)[:, None]).astype(jnp.float32)
    row_ids = jnp.arange(ROWS, dtype=jnp.int32)

    def one_table(table):
        mask = live[table]
        weight = proj[table]

        def one_group(carry, group):
            dp = d_proj[group, :, table, :]
            pl = pooled[group, :, table, :]
            dpool = (jnp.dot(dp, weight.T, preferred_element_type=jnp.float32) * mask[None, :]).astype(jnp.bfloat16)
            plm = jnp.where(mask[None, :] > 0, pl, jnp.zeros_like(pl))
            pgrad = jnp.dot(plm.T, dp, preferred_element_type=jnp.float32)
            counts = jnp.zeros((GROUP_B, ROWS), jnp.float32)
            for slot in range(BAG):
                hit = (bag_rows[group, :, table, slot][:, None] == row_ids[None, :]) & (slot < bag_lengths[group, :, table])[:, None]
                counts = counts + hit.astype(jnp.float32)
            egrad = jnp.dot(counts.astype(jnp.bfloat16).T, dpool, preferred_element_type=jnp.float32)
            return (carry[0] + egrad, carry[1] + pgrad), None

        init = (jnp.zeros((ROWS, EMAX), jnp.float32), jnp.zeros((EMAX, P_SIZE), jnp.float32))
        result, _ = lax.scan(one_group, init, jnp.arange(GROUPS, dtype=jnp.int32))
        return result

    emb_grad, proj_grad = lax.map(one_table, jnp.arange(TABLES, dtype=jnp.int32))
    return emb_grad, proj_grad
```

```python
import functools

import jax
import jax.numpy as jnp
from jax import lax
from jax.experimental import pallas as pl
from jax.experimental.pallas import tpu as pltpu
from jax.sharding import PartitionSpec as P

ROWS = 512
MESH = pl.DeviceIdType.MESH
BF16 = jnp.bfloat16
F32 = jnp.float32


def kernel(
    n_tab,
    n_rep,
    dproj_ref,
    pooled_ref,
    rows_ref,
    lens_ref,
    out_row,
    out_proj,
    dproj_all,
    pooled_all,
    counts,
    own_row,
    own_proj,
    send_row,
    send_proj,
    recv_row,
    recv_proj,
    own_sem,
    a_send,
    a_recv,
    s_send,
    s_recv,
    g_send,
    g_recv,
):
    tab = lax.axis_index("tab")
    rep = lax.axis_index("rep")
    n_samples = dproj_ref.shape[1]
    part = out_row.shape[1]
    n_pair = n_rep // 2
    partner = rep + 1 - 2 * lax.rem(rep, 2)

    def remote(src, dst, send, recv, tab_to, rep_to):
        return pltpu.make_async_remote_copy(
            src_ref=src,
            dst_ref=dst,
            send_sem=send,
            recv_sem=recv,
            device_id=(tab_to, rep_to),
            device_id_type=MESH,
        )

    barrier = pltpu.get_barrier_semaphore()
    for k in range(1, n_tab):
        pl.semaphore_signal(
            barrier, inc=1, device_id=(lax.rem(tab + k, n_tab), rep), device_id_type=MESH
        )
    for k in range(1, n_rep):
        pl.semaphore_signal(
            barrier, inc=1, device_id=(tab, lax.rem(rep + k, n_rep)), device_id_type=MESH
        )
    pl.semaphore_wait(barrier, n_tab + n_rep - 2)

    gathers = []
    for which, (src, dst) in enumerate(((dproj_ref, dproj_all), (pooled_ref, pooled_all))):
        copies = []
        for k in range(1, n_tab):
            to = lax.rem(tab + k, n_tab)
            copy = remote(
                src.at[to], dst.at[tab], a_send.at[which, k], a_recv.at[which, k], to, rep
            )
            copy.start()
            copies.append(copy)
        gathers.append(copies)
    own = [
        pltpu.make_async_copy(src.at[tab], dst.at[tab], own_sem.at[which])
        for which, (src, dst) in enumerate(((dproj_ref, dproj_all), (pooled_ref, pooled_all)))
    ]
    for copy in own:
        copy.start()

    named = rows_ref[...]
    slots = lax.broadcasted_iota(jnp.int32, named.shape, 0)
    named = jnp.where(slots < lens_ref[...], named, -1)
    step = 64

    def count(i, carry):
        at = pl.multiple_of(i * step, step)
        ids = lax.broadcasted_iota(jnp.int32, (step, named.shape[1]), 0) + at
        total = jnp.zeros((step, named.shape[1]), F32)
        for slot in range(named.shape[0]):
            total = total + jnp.where(named[slot : slot + 1, :] == ids, 1.0, 0.0)
        counts[pl.ds(at, step), :] = total.astype(BF16)
        return carry

    lax.fori_loop(0, counts.shape[0] // step, count, 0)

    def scatter(which, partial, own_sum, send, recv):
        own_sum[...] = partial.reshape(own_sum.shape)
        send[...] = partial.reshape(own_sum.shape).astype(BF16)
        copies = []
        for k in range(1, n_rep):
            to = lax.rem(rep + k, n_rep)
            copy = remote(
                send.at[to], recv.at[k], s_send.at[which, k], s_recv.at[which, k], tab, to
            )
            copy.start()
            copies.append(copy)
        return copies

    own[0].wait()
    for copy in gathers[0]:
        copy.wait_recv()
    d_all = dproj_all[...].reshape(n_tab * n_samples, -1)
    row_part = jnp.dot(counts[...], d_all, preferred_element_type=F32)
    row_copies = scatter(0, row_part, own_row, send_row, recv_row)

    own[1].wait()
    for copy in gathers[1]:
        copy.wait_recv()
    p_all = pooled_all[...].reshape(n_tab * n_samples, -1)
    proj_part = lax.dot_general(
        p_all, dproj_all[...].reshape(n_tab * n_samples, -1), (((0,), (0,)), ((), ())),
        preferred_element_type=F32,
    )
    proj_copies = scatter(1, proj_part, own_proj, send_proj, recv_proj)

    def reduce(which, copies, own_sum, recv, out):
        for copy in copies:
            copy.wait_recv()
        total = own_sum[rep]
        for k in range(1, n_rep):
            total = total + recv[k].astype(F32)
        out[rep] = total.astype(BF16)
        started = []
        for k in range(1, n_pair):
            copy = remote(
                out.at[rep], out.at[rep], g_send.at[which, 0, k], g_recv.at[which, 0, k],
                tab, lax.rem(rep + 2 * k, n_rep),
            )
            copy.start()
            started.append(copy)
        pair = remote(
            out.at[rep], out.at[rep], g_send.at[which, 1, 0], g_recv.at[which, 1, 0], tab, partner
        )
        pair.start()
        return started, pair

    def forward(which, started, out):
        copies = []
        for k in range(1, n_pair):
            started[k - 1].wait_recv()
            origin = lax.rem(rep - 2 * k + n_rep, n_rep)
            copy = remote(
                out.at[origin], out.at[origin], g_send.at[which, 1, k], g_recv.at[which, 1, k],
                tab, partner,
            )
            copy.start()
            copies.append(copy)
        return copies

    row_out, row_pair = reduce(0, row_copies, own_row, recv_row, out_row)
    proj_out, proj_pair = reduce(1, proj_copies, own_proj, recv_proj, out_proj)
    row_fwd = forward(0, row_out, out_row)
    proj_fwd = forward(1, proj_out, out_proj)
    for copy in [row_pair, *row_fwd, proj_pair, *proj_fwd]:
        copy.wait()
    for copy in [*gathers[0], *gathers[1], *row_copies, *proj_copies, *row_out, *proj_out]:
        copy.wait_send()


def fused(n_tab, n_rep, d_proj, pooled, proj, bag_rows, bag_lengths, dim_blocks):
    n_samples, width, widest = d_proj.shape[1], d_proj.shape[3], pooled.shape[3]
    group, bag = bag_rows.shape[1], bag_rows.shape[3]
    part, proj_part = ROWS // n_rep, widest // n_rep
    by_table = jnp.transpose(d_proj[0], (1, 0, 2))
    pooled_by_table = jnp.transpose(pooled[0], (1, 0, 2))
    vmem = pl.BlockSpec(memory_space=pltpu.VMEM)
    row_sum, proj_sum = pl.pallas_call(
        functools.partial(kernel, n_tab, n_rep),
        out_shape=(
            jax.ShapeDtypeStruct((n_rep, part, width), BF16),
            jax.ShapeDtypeStruct((n_rep, proj_part, width), BF16),
        ),
        in_specs=[vmem] * 4,
        out_specs=(vmem, vmem),
        scratch_shapes=[
            pltpu.VMEM((n_tab, n_samples, width), BF16),
            pltpu.VMEM((n_tab, n_samples, widest), BF16),
            pltpu.VMEM((ROWS, group), BF16),
            pltpu.VMEM((n_rep, part, width), F32),
            pltpu.VMEM((n_rep, proj_part, width), F32),
            pltpu.VMEM((n_rep, part, width), BF16),
            pltpu.VMEM((n_rep, proj_part, width), BF16),
            pltpu.VMEM((n_rep, part, width), BF16),
            pltpu.VMEM((n_rep, proj_part, width), BF16),
            pltpu.SemaphoreType.DMA((2,)),
            pltpu.SemaphoreType.DMA((2, n_tab)),
            pltpu.SemaphoreType.DMA((2, n_tab)),
            pltpu.SemaphoreType.DMA((2, n_rep)),
            pltpu.SemaphoreType.DMA((2, n_rep)),
            pltpu.SemaphoreType.DMA((2, 2, n_rep // 2)),
            pltpu.SemaphoreType.DMA((2, 2, n_rep // 2)),
        ],
        compiler_params=pltpu.CompilerParams(
            collective_id=0, has_side_effects=True, vmem_limit_bytes=32 << 20
        ),
    )(
        by_table,
        pooled_by_table,
        jnp.transpose(bag_rows[0, :, 0, :]),
        bag_lengths.reshape(1, group),
    )
    tab = lax.axis_index("tab")
    live = jnp.arange(widest, dtype=jnp.int32) < widest // 16 * dim_blocks[tab]
    weight = lax.dynamic_index_in_dim(proj, tab, 0, keepdims=False)
    emb = lax.dot_general(
        row_sum.reshape(ROWS, width), weight, (((1,), (1,)), ((), ())),
        preferred_element_type=F32,
    )
    emb = jnp.where(live[None, :], emb, 0.0)
    proj_grad = jnp.where(live[:, None], proj_sum.reshape(widest, width).astype(F32), 0.0)
    return emb[None], proj_grad[None]


def general(d_proj, pooled, proj, bag_rows, bag_lengths, dim_blocks):
    widest = proj.shape[1]
    group_rows = bag_rows.shape[1]
    bag_size = bag_rows.shape[3]
    columns = jnp.arange(widest, dtype=jnp.int32)
    live = (columns[None, :] < (widest // 16 * dim_blocks)[:, None]).astype(F32)
    samples_proj = d_proj[0]
    masked_pool = jnp.where(live[None, :, :] > 0, pooled[0], jnp.zeros_like(pooled[0]))
    proj_part = lax.psum_scatter(
        jnp.einsum("bte,btp->tep", masked_pool, samples_proj, preferred_element_type=F32),
        "tab",
        scatter_dimension=0,
        tiled=True,
    )
    back = jnp.einsum("btp,tep->bte", samples_proj, proj, preferred_element_type=F32)
    back = (back * live[None, :, :]).astype(BF16)
    d_pooled = lax.all_to_all(back, "tab", split_axis=1, concat_axis=0, tiled=True)
    row_ids = jnp.arange(ROWS, dtype=jnp.int32)
    counts = jnp.zeros((group_rows, ROWS), F32)
    for slot in range(bag_size):
        hit = (bag_rows[0, :, 0, slot][:, None] == row_ids[None, :]) & (
            slot < bag_lengths[0, :, 0]
        )[:, None]
        counts = counts + hit.astype(F32)
    emb_part = lax.dot_general(
        counts.astype(BF16), d_pooled[:, 0, :], (((0,), (0,)), ((), ())),
        preferred_element_type=F32,
    )
    return lax.psum((emb_part[None], proj_part), "rep")


def solution(mesh):
    n_tab, n_rep = mesh.shape["tab"], mesh.shape["rep"]
    placed = (
        P("rep", "tab", None, None),
        P("rep", "tab", None, None),
        P(),
        P("rep", None, "tab", None),
        P("rep", None, "tab"),
        P(),
    )

    def body(*args):
        if n_rep % 2 == 0 and ROWS % (16 * n_rep) == 0 and args[2].shape[1] % (16 * n_rep) == 0:
            return fused(n_tab, n_rep, *args)
        return general(*args)

    return jax.shard_map(
        body,
        mesh=mesh,
        in_specs=placed,
        out_specs=(P("tab", None, None), P("tab", None, None)),
        check_vma=False,
    )
```

```python
import functools

import jax
import jax.numpy as jnp
from jax import lax
from jax.experimental import pallas as pl
from jax.experimental.pallas import tpu as pltpu
from jax.sharding import PartitionSpec as P

ROWS = 512
MESH = pl.DeviceIdType.MESH
BF16 = jnp.bfloat16
F32 = jnp.float32


def kernel(
    n_tab,
    n_rep,
    dproj_ref,
    pooled_ref,
    rows_hbm,
    lens_hbm,
    out_row,
    out_proj,
    rows_ref,
    lens_ref,
    dproj_all,
    pooled_all,
    counts,
    row_own,
    row_wire,
    proj_own,
    proj_wire,
    own_sem,
    a_send,
    a_recv,
    y_send,
    y_recv,
    z_send,
    z_recv,
    g_send,
    g_recv,
):
    tab = lax.axis_index("tab")
    rep = lax.axis_index("rep")
    n_z = n_rep // 2
    y = lax.rem(rep, 2)
    z = rep // 2
    partner = rep + 1 - 2 * y
    n_samples, width = dproj_ref.shape[1], dproj_ref.shape[2]
    piece = pooled_ref.shape[2] // 2

    def remote(src, dst, send, recv, tab_to, rep_to):
        return pltpu.make_async_remote_copy(
            src_ref=src,
            dst_ref=dst,
            send_sem=send,
            recv_sem=recv,
            device_id=(tab_to, rep_to),
            device_id_type=MESH,
        )

    barrier = pltpu.get_barrier_semaphore()
    for k in range(1, n_tab):
        pl.semaphore_signal(
            barrier, inc=1, device_id=(lax.rem(tab + k, n_tab), rep), device_id_type=MESH
        )
    for k in range(1, n_z):
        pl.semaphore_signal(
            barrier, inc=1, device_id=(tab, lax.rem(rep + 2 * k, n_rep)), device_id_type=MESH
        )
    pl.semaphore_signal(barrier, inc=1, device_id=(tab, partner), device_id_type=MESH)
    bags = [
        pltpu.make_async_copy(rows_hbm, rows_ref, own_sem.at[2]),
        pltpu.make_async_copy(lens_hbm, lens_ref, own_sem.at[3]),
    ]
    for copy in bags:
        copy.start()
    pl.semaphore_wait(barrier, n_tab - 1 + n_z)

    def columns(ref, at, which):
        return ref.at[at] if which == 0 else ref.at[at, :, pl.ds((which - 1) * piece, piece)]

    gathers = []
    for which in range(3):
        src, dst = (dproj_ref, dproj_all) if which == 0 else (pooled_ref, pooled_all)
        copies = []
        for k in range(1, n_tab):
            to = lax.rem(tab + k, n_tab)
            copy = remote(
                columns(src, to, which), columns(dst, tab, which),
                a_send.at[which, k], a_recv.at[which, k], to, rep,
            )
            copy.start()
            copies.append(copy)
        gathers.append(copies)
    own = [
        pltpu.make_async_copy(src.at[tab], dst.at[tab], own_sem.at[which])
        for which, (src, dst) in enumerate(((dproj_ref, dproj_all), (pooled_ref, pooled_all)))
    ]
    for copy in own:
        copy.start()

    for copy in bags:
        copy.wait()
    named = rows_ref[...]
    slots = lax.broadcasted_iota(jnp.int32, named.shape, 0)
    named = jnp.where(slots < lens_ref[...], named, -1)
    step = 64

    def count(i, carry):
        at = pl.multiple_of(i * step, step)
        ids = lax.broadcasted_iota(jnp.int32, (step, named.shape[1]), 0) + at
        total = jnp.zeros((step, named.shape[1]), F32)
        for slot in range(named.shape[0]):
            total = total + jnp.where(named[slot : slot + 1, :] == ids, 1.0, 0.0)
        counts[pl.ds(at, step), :] = total.astype(BF16)
        return carry

    lax.fori_loop(0, counts.shape[0] // step, count, 0)

    buffers = [
        (row_own, row_wire, out_row),
        (proj_own.at[0], proj_wire.at[0], out_proj.at[0]),
        (proj_own.at[1], proj_wire.at[1], out_proj.at[1]),
    ]

    def send_pair(which):
        sums, wire, _ = buffers[which]
        wire[0] = sums[1 - y].astype(BF16)
        copy = remote(wire.at[0], wire.at[1], y_send.at[which], y_recv.at[which], tab, partner)
        copy.start()
        return copy

    def send_line(which, pair):
        sums, wire, _ = buffers[which]
        pair.wait_recv()
        total = sums[y] + wire[1].astype(F32)
        wire[2] = total.astype(BF16)
        copies = []
        for k in range(1, n_z):
            to = lax.rem(z + k, n_z)
            copy = remote(
                wire.at[2, to], wire.at[3, k], z_send.at[which, k], z_recv.at[which, k],
                tab, 2 * to + y,
            )
            copy.start()
            copies.append(copy)
        sums[y] = total
        return copies

    def send_sums(which, line):
        sums, wire, out = buffers[which]
        for copy in line:
            copy.wait_recv()
        total = sums[y, z]
        for k in range(1, n_z):
            total = total + wire[3, k].astype(F32)
        high = total.astype(BF16)
        if which == 0:
            out[y, z, :, :width] = high
            out[y, z, :, width:] = (total - high.astype(F32)).astype(BF16)
        else:
            out[y, z] = high
        block = out.at[y, z]
        copies = []
        for k in range(1, n_z):
            copy = remote(
                block, block, g_send.at[which, 0, k], g_recv.at[which, 0, k],
                tab, 2 * lax.rem(z + k, n_z) + y,
            )
            copy.start()
            copies.append(copy)
        copy = remote(
            block, block, g_send.at[which, 1, 0], g_recv.at[which, 1, 0], tab, partner
        )
        copy.start()
        return copies, copy

    def forward(which, arriving):
        out = buffers[which][2]
        copies = []
        for k in range(1, n_z):
            arriving[k - 1].wait_recv()
            block = out.at[y, lax.rem(z - k + n_z, n_z)]
            copy = remote(
                block, block, g_send.at[which, 1, k], g_recv.at[which, 1, k], tab, partner
            )
            copy.start()
            copies.append(copy)
        return copies

    def project(half):
        total = None
        for k in range(n_tab):
            if k > 0:
                gathers[1 + half][k - 1].wait_recv()
            at = lax.rem(tab - k + n_tab, n_tab)
            term = lax.dot_general(
                pooled_all[at, :, half * piece : (half + 1) * piece], dproj_all[at],
                (((0,), (0,)), ((), ())), preferred_element_type=F32,
            )
            total = term if total is None else total + term
        proj_own[half] = total.reshape(proj_own.shape[1:])
        return send_pair(1 + half)

    own[0].wait()
    for copy in gathers[0]:
        copy.wait_recv()
    d_all = dproj_all[...].reshape(n_tab * n_samples, width)
    row_own[...] = jnp.dot(counts[...], d_all, preferred_element_type=F32).reshape(row_own.shape)
    pair0 = send_pair(0)
    own[1].wait()
    pair1 = project(0)
    line0 = send_line(0, pair0)
    pair2 = project(1)
    line1 = send_line(1, pair1)
    line2 = send_line(2, pair2)
    sums0, last0 = send_sums(0, line0)
    sums1, last1 = send_sums(1, line1)
    sums2, last2 = send_sums(2, line2)
    fwd0 = forward(0, sums0)
    fwd1 = forward(1, sums1)
    fwd2 = forward(2, sums2)
    for copy in [last0, *fwd0, last1, *fwd1, last2, *fwd2]:
        copy.wait()
    for copy in [
        *gathers[0], *gathers[1], *gathers[2], pair0, pair1, pair2,
        *line0, *line1, *line2, *sums0, *sums1, *sums2,
    ]:
        copy.wait_send()


def finish(dims_ref, row_ref, sum_ref, weight_ref, emb_ref, proj_ref):
    tab = lax.axis_index("tab")
    widest = weight_ref.shape[1]
    limit = widest // 16 * dims_ref[tab]
    weight = weight_ref[tab]
    width = weight.shape[1]
    rows = row_ref[...]
    emb = lax.dot_general(
        rows[:, :width], weight, (((1,), (1,)), ((), ())), preferred_element_type=F32
    ) + lax.dot_general(
        rows[:, width:], weight, (((1,), (1,)), ((), ())), preferred_element_type=F32
    )
    emb_ref[0] = jnp.where(lax.broadcasted_iota(jnp.int32, emb.shape, 1) < limit, emb, 0.0)
    total = sum_ref[...].astype(F32)
    at = lax.broadcasted_iota(jnp.int32, total.shape, 0) + pl.program_id(0) * total.shape[0]
    proj_ref[0] = jnp.where(at < limit, total, 0.0)


def fused(n_tab, n_rep, d_proj, pooled, proj, bag_rows, bag_lengths, dim_blocks):
    n_samples, width, widest = d_proj.shape[1], d_proj.shape[3], pooled.shape[3]
    group, bag = bag_rows.shape[1], bag_rows.shape[3]
    n_z = n_rep // 2
    part, proj_part = ROWS // n_rep, widest // 2 // n_rep
    by_table = jnp.transpose(d_proj[0], (1, 0, 2))
    pooled_by_table = jnp.transpose(pooled[0], (1, 0, 2))
    vmem = pl.BlockSpec(memory_space=pltpu.VMEM)
    hbm = pl.BlockSpec(memory_space=pl.ANY)
    dma = pltpu.SemaphoreType.DMA
    row_sum, proj_sum = pl.pallas_call(
        functools.partial(kernel, n_tab, n_rep),
        out_shape=(
            jax.ShapeDtypeStruct((2, n_z, part, 2 * width), BF16),
            jax.ShapeDtypeStruct((2, 2, n_z, proj_part, width), BF16),
        ),
        in_specs=[vmem, vmem, hbm, hbm],
        out_specs=(vmem, vmem),
        scratch_shapes=[
            pltpu.VMEM((bag, group), jnp.int32),
            pltpu.VMEM((1, group), jnp.int32),
            pltpu.VMEM((n_tab, n_samples, width), BF16),
            pltpu.VMEM((n_tab, n_samples, widest), BF16),
            pltpu.VMEM((ROWS, group), BF16),
            pltpu.VMEM((2, n_z, part, width), F32),
            pltpu.VMEM((4, n_z, part, width), BF16),
            pltpu.VMEM((2, 2, n_z, proj_part, width), F32),
            pltpu.VMEM((2, 4, n_z, proj_part, width), BF16),
            dma((4,)),
            dma((3, n_tab)),
            dma((3, n_tab)),
            dma((3,)),
            dma((3,)),
            dma((3, n_z)),
            dma((3, n_z)),
            dma((3, 2, n_z)),
            dma((3, 2, n_z)),
        ],
        compiler_params=pltpu.CompilerParams(
            collective_id=0, has_side_effects=True, vmem_limit_bytes=32 << 20
        ),
    )(
        by_table,
        pooled_by_table,
        jnp.transpose(bag_rows[0, :, 0, :]),
        bag_lengths.reshape(1, group),
    )
    tiles = 4
    emb, proj_grad = pl.pallas_call(
        finish,
        grid=(tiles,),
        out_shape=(
            jax.ShapeDtypeStruct((1, ROWS, widest), F32),
            jax.ShapeDtypeStruct((1, widest, width), F32),
        ),
        in_specs=[
            pl.BlockSpec(memory_space=pltpu.SMEM),
            pl.BlockSpec((ROWS // tiles, 2 * width), lambda i: (i, 0)),
            pl.BlockSpec((widest // tiles, width), lambda i: (i, 0)),
            vmem,
        ],
        out_specs=(
            pl.BlockSpec((1, ROWS // tiles, widest), lambda i: (0, i, 0)),
            pl.BlockSpec((1, widest // tiles, width), lambda i: (0, i, 0)),
        ),
        compiler_params=pltpu.CompilerParams(vmem_limit_bytes=16 << 20),
        cost_estimate=pl.CostEstimate(
            flops=4 * ROWS * widest * width,
            bytes_accessed=4 * ROWS * widest + 6 * widest * width,
            transcendentals=0,
        ),
    )(dim_blocks, row_sum.reshape(ROWS, 2 * width), proj_sum.reshape(widest, width), proj)
    return emb, proj_grad


def general(d_proj, pooled, proj, bag_rows, bag_lengths, dim_blocks):
    widest = proj.shape[1]
    group_rows = bag_rows.shape[1]
    bag_size = bag_rows.shape[3]
    columns = jnp.arange(widest, dtype=jnp.int32)
    live = (columns[None, :] < (widest // 16 * dim_blocks)[:, None]).astype(F32)
    samples_proj = d_proj[0]
    masked_pool = jnp.where(live[None, :, :] > 0, pooled[0], jnp.zeros_like(pooled[0]))
    proj_part = lax.psum_scatter(
        jnp.einsum("bte,btp->tep", masked_pool, samples_proj, preferred_element_type=F32),
        "tab",
        scatter_dimension=0,
        tiled=True,
    )
    back = jnp.einsum("btp,tep->bte", samples_proj, proj, preferred_element_type=F32)
    back = (back * live[None, :, :]).astype(BF16)
    d_pooled = lax.all_to_all(back, "tab", split_axis=1, concat_axis=0, tiled=True)
    row_ids = jnp.arange(ROWS, dtype=jnp.int32)
    counts = jnp.zeros((group_rows, ROWS), F32)
    for slot in range(bag_size):
        hit = (bag_rows[0, :, 0, slot][:, None] == row_ids[None, :]) & (
            slot < bag_lengths[0, :, 0]
        )[:, None]
        counts = counts + hit.astype(F32)
    emb_part = lax.dot_general(
        counts.astype(BF16), d_pooled[:, 0, :], (((0,), (0,)), ((), ())),
        preferred_element_type=F32,
    )
    return lax.psum((emb_part[None], proj_part), "rep")


def solution(mesh):
    n_tab, n_rep = mesh.shape["tab"], mesh.shape["rep"]
    placed = (
        P("rep", "tab", None, None),
        P("rep", "tab", None, None),
        P(),
        P("rep", None, "tab", None),
        P("rep", None, "tab"),
        P(),
    )

    def body(*args):
        if n_rep % 2 == 0 and ROWS % (16 * n_rep) == 0 and args[2].shape[1] % (32 * n_rep) == 0:
            return fused(n_tab, n_rep, *args)
        return general(*args)

    return jax.shard_map(
        body,
        mesh=mesh,
        in_specs=placed,
        out_specs=(P("tab", None, None), P("tab", None, None)),
        check_vma=False,
    )
```

```python
import functools

import jax
import jax.numpy as jnp
from jax import lax
from jax.experimental import pallas as pl
from jax.experimental.pallas import tpu as pltpu
from jax.sharding import PartitionSpec as P

ROWS = 512
MESH = pl.DeviceIdType.MESH
BF16 = jnp.bfloat16
F32 = jnp.float32


def kernel(
    n_tab,
    n_rep,
    dproj_hbm,
    pooled_hbm,
    rows_hbm,
    lens_hbm,
    weight_hbm,
    dims_hbm,
    out_row,
    out_proj,
    out_weight,
    row_sum,
    proj_sum,
    live_weight,
    dproj_raw,
    pooled_raw,
    dproj_ref,
    pooled_ref,
    rows_ref,
    lens_ref,
    weight_ref,
    dims_ref,
    dproj_all,
    pooled_all,
    counts,
    row_own,
    row_wire,
    proj_own,
    proj_wire,
    load_sem,
    store_sem,
    own_sem,
    a_send,
    a_recv,
    y_send,
    y_recv,
    z_send,
    z_recv,
    g_send,
    g_recv,
):
    tab = lax.axis_index("tab")
    rep = lax.axis_index("rep")
    n_z = n_rep // 2
    y = lax.rem(rep, 2)
    z = rep // 2
    partner = rep + 1 - 2 * y
    n_samples, width = dproj_ref.shape[1], dproj_ref.shape[2]
    piece = pooled_ref.shape[2] // 2

    loads = [
        pltpu.make_async_copy(src, dst, load_sem.at[i])
        for i, (src, dst) in enumerate((
            (dproj_hbm, dproj_raw),
            (pooled_hbm, pooled_raw),
            (rows_hbm, rows_ref),
            (lens_hbm, lens_ref),
            (weight_hbm.at[tab], weight_ref),
            (dims_hbm, dims_ref),
        ))
    ]
    for copy in loads:
        copy.start()

    def remote(src, dst, send, recv, tab_to, rep_to):
        return pltpu.make_async_remote_copy(
            src_ref=src,
            dst_ref=dst,
            send_sem=send,
            recv_sem=recv,
            device_id=(tab_to, rep_to),
            device_id_type=MESH,
        )

    barrier = pltpu.get_barrier_semaphore()
    for k in range(1, n_tab):
        pl.semaphore_signal(
            barrier, inc=1, device_id=(lax.rem(tab + k, n_tab), rep), device_id_type=MESH
        )
    for k in range(1, n_z):
        pl.semaphore_signal(
            barrier, inc=1, device_id=(tab, lax.rem(rep + 2 * k, n_rep)), device_id_type=MESH
        )
    pl.semaphore_signal(barrier, inc=1, device_id=(tab, partner), device_id_type=MESH)
    loads[0].wait()
    dproj_ref[...] = jnp.transpose(dproj_raw[...], (1, 0, 2))
    pl.semaphore_wait(barrier, n_tab - 1 + n_z)

    def columns(ref, at, which):
        return ref.at[at] if which == 0 else ref.at[at, :, pl.ds((which - 1) * piece, piece)]

    gathers = []
    for which in range(3):
        if which == 1:
            loads[1].wait()
            pooled_ref[...] = jnp.transpose(pooled_raw[...], (1, 0, 2))
        src, dst = (dproj_ref, dproj_all) if which == 0 else (pooled_ref, pooled_all)
        copies = []
        for k in range(1, n_tab):
            to = lax.rem(tab + k, n_tab)
            copy = remote(
                columns(src, to, which), columns(dst, tab, which),
                a_send.at[which, k], a_recv.at[which, k], to, rep,
            )
            copy.start()
            copies.append(copy)
        gathers.append(copies)
    own = [
        pltpu.make_async_copy(src.at[tab], dst.at[tab], own_sem.at[which])
        for which, (src, dst) in enumerate(((dproj_ref, dproj_all), (pooled_ref, pooled_all)))
    ]
    for copy in own:
        copy.start()

    for copy in loads[2:4]:
        copy.wait()
    named = rows_ref[...]
    slots = lax.broadcasted_iota(jnp.int32, named.shape, 0)
    named = jnp.where(slots < lens_ref[...], named, -1)
    step = 64

    def count(i, carry):
        at = pl.multiple_of(i * step, step)
        ids = lax.broadcasted_iota(jnp.int32, (step, named.shape[1]), 0) + at
        total = jnp.zeros((step, named.shape[1]), F32)
        for slot in range(named.shape[0]):
            total = total + jnp.where(named[slot : slot + 1, :] == ids, 1.0, 0.0)
        counts[pl.ds(at, step), :] = total.astype(BF16)
        return carry

    lax.fori_loop(0, counts.shape[0] // step, count, 0)

    buffers = [
        (row_own, row_wire, row_sum),
        (proj_own.at[0], proj_wire.at[0], proj_sum.at[0]),
        (proj_own.at[1], proj_wire.at[1], proj_sum.at[1]),
    ]

    def send_pair(which):
        sums, wire, _ = buffers[which]
        wire[0] = sums[1 - y].astype(BF16)
        copy = remote(wire.at[0], wire.at[1], y_send.at[which], y_recv.at[which], tab, partner)
        copy.start()
        return copy

    def send_line(which, pair):
        sums, wire, _ = buffers[which]
        pair.wait_recv()
        total = sums[y] + wire[1].astype(F32)
        wire[2] = total.astype(BF16)
        copies = []
        for k in range(1, n_z):
            to = lax.rem(z + k, n_z)
            copy = remote(
                wire.at[2, to], wire.at[3, k], z_send.at[which, k], z_recv.at[which, k],
                tab, 2 * to + y,
            )
            copy.start()
            copies.append(copy)
        sums[y] = total
        return copies

    def send_sums(which, line):
        sums, wire, out = buffers[which]
        for copy in line:
            copy.wait_recv()
        total = sums[y, z]
        for k in range(1, n_z):
            total = total + wire[3, k].astype(F32)
        high = total.astype(BF16)
        if which == 0:
            out[y, z, :, :width] = high
            out[y, z, :, width:] = (total - high.astype(F32)).astype(BF16)
        else:
            first = (which - 1) * piece + (y * n_z + z) * total.shape[0]
            at = lax.broadcasted_iota(jnp.int32, total.shape, 0) + first
            out[y, z] = jnp.where(at < limit, total, 0.0).astype(BF16)
        block = out.at[y, z]
        copies = []
        for k in range(1, n_z):
            copy = remote(
                block, block, g_send.at[which, 0, k], g_recv.at[which, 0, k],
                tab, 2 * lax.rem(z + k, n_z) + y,
            )
            copy.start()
            copies.append(copy)
        copy = remote(
            block, block, g_send.at[which, 1, 0], g_recv.at[which, 1, 0], tab, partner
        )
        copy.start()
        return copies, copy

    def forward(which, arriving):
        out = buffers[which][2]
        copies = []
        for k in range(1, n_z):
            arriving[k - 1].wait_recv()
            block = out.at[y, lax.rem(z - k + n_z, n_z)]
            copy = remote(
                block, block, g_send.at[which, 1, k], g_recv.at[which, 1, k], tab, partner
            )
            copy.start()
            copies.append(copy)
        return copies

    def project(half):
        total = None
        for k in range(n_tab):
            if k > 0:
                gathers[1 + half][k - 1].wait_recv()
            at = lax.rem(tab - k + n_tab, n_tab)
            term = lax.dot_general(
                pooled_all[at, :, half * piece : (half + 1) * piece], dproj_all[at],
                (((0,), (0,)), ((), ())), preferred_element_type=F32,
            )
            total = term if total is None else total + term
        proj_own[half] = total.reshape(proj_own.shape[1:])
        return send_pair(1 + half)

    for copy in loads[4:]:
        copy.wait()
    limit = weight_ref.shape[0] // 16 * dims_ref[tab]
    at_row = lax.broadcasted_iota(jnp.int32, weight_ref.shape, 0)
    live_weight[...] = jnp.where(at_row < limit, weight_ref[...].astype(F32), 0.0).astype(BF16)
    stores = [
        pltpu.make_async_copy(src, dst, store_sem.at[i])
        for i, (src, dst) in enumerate((
            (live_weight, out_weight),
            (row_sum, out_row),
            (proj_sum.at[0], out_proj.at[0]),
            (proj_sum.at[1], out_proj.at[1]),
        ))
    ]
    stores[0].start()

    own[0].wait()
    for copy in gathers[0]:
        copy.wait_recv()
    d_all = dproj_all[...].reshape(n_tab * n_samples, width)
    row_own[...] = jnp.dot(counts[...], d_all, preferred_element_type=F32).reshape(row_own.shape)
    pair0 = send_pair(0)
    own[1].wait()
    pair1 = project(0)
    line0 = send_line(0, pair0)
    pair2 = project(1)
    line1 = send_line(1, pair1)
    line2 = send_line(2, pair2)
    sums0, last0 = send_sums(0, line0)
    sums1, last1 = send_sums(1, line1)
    sums2, last2 = send_sums(2, line2)
    fwd0 = forward(0, sums0)
    fwd1 = forward(1, sums1)
    fwd2 = forward(2, sums2)
    for i, copies in enumerate(([last0, *fwd0], [last1, *fwd1], [last2, *fwd2])):
        for copy in copies:
            copy.wait_recv()
        stores[1 + i].start()
    for copy in [
        *gathers[0], *gathers[1], *gathers[2], pair0, pair1, pair2,
        *line0, *line1, *line2, *sums0, *sums1, *sums2,
        last0, last1, last2, *fwd0, *fwd1, *fwd2,
    ]:
        copy.wait_send()
    for copy in stores:
        copy.wait()


def finish(
    row_hbm, sum_hbm, weight_hbm, emb_hbm, proj_hbm,
    row_ref, sum_ref, weight_ref, emb_buf, proj_buf, load_sem, sem,
):
    loads = [
        pltpu.make_async_copy(src, dst, load_sem.at[i])
        for i, (src, dst) in enumerate((
            (sum_hbm, sum_ref), (weight_hbm, weight_ref), (row_hbm, row_ref)
        ))
    ]
    for copy in loads:
        copy.start()
    width = weight_ref.shape[1]
    tiles = emb_buf.shape[0]
    tile = emb_buf.shape[1]
    copies = []

    def store(buf, hbm, i):
        copy = pltpu.make_async_copy(buf, hbm, sem.at[i])
        copy.start()
        copies.append(copy)

    loads[0].wait()
    proj_buf[...] = sum_ref[...].astype(F32)
    store(proj_buf, proj_hbm.at[0], tiles)
    loads[1].wait()
    loads[2].wait()
    weight = weight_ref[...]
    for i in range(tiles):
        rows = row_ref[i * tile : (i + 1) * tile, :]
        emb_buf[i] = lax.dot_general(
            rows[:, :width], weight, (((1,), (1,)), ((), ())), preferred_element_type=F32
        ) + lax.dot_general(
            rows[:, width:], weight, (((1,), (1,)), ((), ())), preferred_element_type=F32
        )
        store(emb_buf.at[i], emb_hbm.at[0, pl.ds(i * tile, tile)], i)
    for copy in copies:
        copy.wait()


def fused(n_tab, n_rep, d_proj, pooled, proj, bag_rows, bag_lengths, dim_blocks):
    n_samples, width, widest = d_proj.shape[1], d_proj.shape[3], pooled.shape[3]
    group, bag = bag_rows.shape[1], bag_rows.shape[3]
    n_z = n_rep // 2
    part, proj_part = ROWS // n_rep, widest // 2 // n_rep
    hbm = pl.BlockSpec(memory_space=pltpu.HBM)
    dma = pltpu.SemaphoreType.DMA
    row_sum, proj_sum, weight = pl.pallas_call(
        functools.partial(kernel, n_tab, n_rep),
        out_shape=(
            jax.ShapeDtypeStruct((2, n_z, part, 2 * width), BF16),
            jax.ShapeDtypeStruct((2, 2, n_z, proj_part, width), BF16),
            jax.ShapeDtypeStruct((widest, width), BF16),
        ),
        in_specs=[hbm] * 6,
        out_specs=(hbm, hbm, hbm),
        scratch_shapes=[
            pltpu.VMEM((2, n_z, part, 2 * width), BF16),
            pltpu.VMEM((2, 2, n_z, proj_part, width), BF16),
            pltpu.VMEM((widest, width), BF16),
            pltpu.VMEM((n_samples, n_tab, width), BF16),
            pltpu.VMEM((n_samples, n_tab, widest), BF16),
            pltpu.VMEM((n_tab, n_samples, width), BF16),
            pltpu.VMEM((n_tab, n_samples, widest), BF16),
            pltpu.VMEM((bag, group), jnp.int32),
            pltpu.VMEM((1, group), jnp.int32),
            pltpu.VMEM((widest, width), BF16),
            pltpu.SMEM((n_tab,), jnp.int32),
            pltpu.VMEM((n_tab, n_samples, width), BF16),
            pltpu.VMEM((n_tab, n_samples, widest), BF16),
            pltpu.VMEM((ROWS, group), BF16),
            pltpu.VMEM((2, n_z, part, width), F32),
            pltpu.VMEM((4, n_z, part, width), BF16),
            pltpu.VMEM((2, 2, n_z, proj_part, width), F32),
            pltpu.VMEM((2, 4, n_z, proj_part, width), BF16),
            dma((6,)),
            dma((4,)),
            dma((2,)),
            dma((3, n_tab)),
            dma((3, n_tab)),
            dma((3,)),
            dma((3,)),
            dma((3, n_z)),
            dma((3, n_z)),
            dma((3, 2, n_z)),
            dma((3, 2, n_z)),
        ],
        compiler_params=pltpu.CompilerParams(
            collective_id=0, has_side_effects=True, vmem_limit_bytes=60 << 20
        ),
    )(
        d_proj[0],
        pooled[0],
        jnp.transpose(bag_rows[0, :, 0, :]),
        bag_lengths.reshape(1, group),
        proj,
        dim_blocks,
    )
    tiles = 4
    emb, proj_grad = pl.pallas_call(
        finish,
        out_shape=(
            jax.ShapeDtypeStruct((1, ROWS, widest), F32),
            jax.ShapeDtypeStruct((1, widest, width), F32),
        ),
        in_specs=[hbm] * 3,
        out_specs=(hbm, hbm),
        scratch_shapes=[
            pltpu.VMEM((ROWS, 2 * width), BF16),
            pltpu.VMEM((widest, width), BF16),
            pltpu.VMEM((widest, width), BF16),
            pltpu.VMEM((tiles, ROWS // tiles, widest), F32),
            pltpu.VMEM((widest, width), F32),
            dma((3,)),
            dma((tiles + 1,)),
        ],
        compiler_params=pltpu.CompilerParams(vmem_limit_bytes=60 << 20),
        cost_estimate=pl.CostEstimate(
            flops=4 * ROWS * widest * width,
            bytes_accessed=4 * ROWS * widest + 6 * widest * width,
            transcendentals=0,
        ),
    )(row_sum.reshape(ROWS, 2 * width), proj_sum.reshape(widest, width), weight)
    return emb, proj_grad


def general(d_proj, pooled, proj, bag_rows, bag_lengths, dim_blocks):
    widest = proj.shape[1]
    group_rows = bag_rows.shape[1]
    bag_size = bag_rows.shape[3]
    columns = jnp.arange(widest, dtype=jnp.int32)
    live = (columns[None, :] < (widest // 16 * dim_blocks)[:, None]).astype(F32)
    samples_proj = d_proj[0]
    masked_pool = jnp.where(live[None, :, :] > 0, pooled[0], jnp.zeros_like(pooled[0]))
    proj_part = lax.psum_scatter(
        jnp.einsum("bte,btp->tep", masked_pool, samples_proj, preferred_element_type=F32),
        "tab",
        scatter_dimension=0,
        tiled=True,
    )
    back = jnp.einsum("btp,tep->bte", samples_proj, proj, preferred_element_type=F32)
    back = (back * live[None, :, :]).astype(BF16)
    d_pooled = lax.all_to_all(back, "tab", split_axis=1, concat_axis=0, tiled=True)
    row_ids = jnp.arange(ROWS, dtype=jnp.int32)
    counts = jnp.zeros((group_rows, ROWS), F32)
    for slot in range(bag_size):
        hit = (bag_rows[0, :, 0, slot][:, None] == row_ids[None, :]) & (
            slot < bag_lengths[0, :, 0]
        )[:, None]
        counts = counts + hit.astype(F32)
    emb_part = lax.dot_general(
        counts.astype(BF16), d_pooled[:, 0, :], (((0,), (0,)), ((), ())),
        preferred_element_type=F32,
    )
    return lax.psum((emb_part[None], proj_part), "rep")


def solution(mesh):
    n_tab, n_rep = mesh.shape["tab"], mesh.shape["rep"]
    placed = (
        P("rep", "tab", None, None),
        P("rep", "tab", None, None),
        P(),
        P("rep", None, "tab", None),
        P("rep", None, "tab"),
        P(),
    )

    def body(*args):
        if n_rep % 2 == 0 and ROWS % (16 * n_rep) == 0 and args[2].shape[1] % (32 * n_rep) == 0:
            return fused(n_tab, n_rep, *args)
        return general(*args)

    return jax.shard_map(
        body,
        mesh=mesh,
        in_specs=placed,
        out_specs=(P("tab", None, None), P("tab", None, None)),
        check_vma=False,
    )
```

```python
import functools

import jax
import jax.numpy as jnp
from jax import lax
from jax.experimental import pallas as pl
from jax.experimental.pallas import tpu as pltpu
from jax.sharding import PartitionSpec as P

ROWS = 512
MESH = pl.DeviceIdType.MESH
BF16 = jnp.bfloat16
F32 = jnp.float32


SCALE_ROWS = 16


def encode(total):
    peak = jnp.maximum(jnp.max(jnp.abs(total), axis=0, keepdims=True), 1e-30)
    power = jnp.floor(jnp.log2(peak) + 1.01) - 15.0
    coded = jnp.floor(total * jnp.exp2(-power) + 0.5)
    coded = jnp.clip(coded, -32767.0, 32767.0).astype(jnp.int32).astype(jnp.int16)
    powers = jnp.broadcast_to(power, (SCALE_ROWS, total.shape[1]))
    return coded, powers.astype(jnp.int32).astype(jnp.int16)


def decode(coded, powers):
    scale = jnp.exp2(powers.astype(jnp.int32).astype(F32)[:1])
    return coded.astype(jnp.int32).astype(F32) * scale


def kernel(
    n_tab,
    n_rep,
    dproj_hbm,
    pooled_hbm,
    rows_hbm,
    lens_hbm,
    weight_hbm,
    dims_hbm,
    out_emb,
    out_proj,
    row_sum,
    proj_sum,
    emb_buf,
    proj_buf,
    live_weight,
    dproj_raw,
    pooled_raw,
    dproj_ref,
    pooled_ref,
    rows_ref,
    lens_ref,
    weight_ref,
    dims_ref,
    dproj_all,
    pooled_all,
    counts,
    row_own,
    row_wire,
    proj_own,
    proj_wire,
    load_sem,
    store_sem,
    own_sem,
    a_send,
    a_recv,
    y_send,
    y_recv,
    z_send,
    z_recv,
    g_send,
    g_recv,
):
    tab = lax.axis_index("tab")
    rep = lax.axis_index("rep")
    n_z = n_rep // 2
    y = lax.rem(rep, 2)
    z = rep // 2
    partner = rep + 1 - 2 * y
    n_samples, width = dproj_ref.shape[1], dproj_ref.shape[2]
    piece = pooled_ref.shape[2] // 2

    loads = [
        pltpu.make_async_copy(src, dst, load_sem.at[i])
        for i, (src, dst) in enumerate((
            (dproj_hbm, dproj_raw),
            (pooled_hbm, pooled_raw),
            (rows_hbm, rows_ref),
            (lens_hbm, lens_ref),
            (weight_hbm.at[tab], weight_ref),
            (dims_hbm, dims_ref),
        ))
    ]
    for copy in loads:
        copy.start()

    def remote(src, dst, send, recv, tab_to, rep_to):
        return pltpu.make_async_remote_copy(
            src_ref=src,
            dst_ref=dst,
            send_sem=send,
            recv_sem=recv,
            device_id=(tab_to, rep_to),
            device_id_type=MESH,
        )

    barrier = pltpu.get_barrier_semaphore()
    for k in range(1, n_tab):
        pl.semaphore_signal(
            barrier, inc=1, device_id=(lax.rem(tab + k, n_tab), rep), device_id_type=MESH
        )
    for k in range(1, n_z):
        pl.semaphore_signal(
            barrier, inc=1, device_id=(tab, lax.rem(rep + 2 * k, n_rep)), device_id_type=MESH
        )
    pl.semaphore_signal(barrier, inc=1, device_id=(tab, partner), device_id_type=MESH)
    loads[0].wait()
    dproj_ref[...] = jnp.transpose(dproj_raw[...], (1, 0, 2))
    pl.semaphore_wait(barrier, n_tab - 1 + n_z)

    def columns(ref, at, which):
        return ref.at[at] if which == 0 else ref.at[at, :, pl.ds((which - 1) * piece, piece)]

    gathers = []
    for which in range(3):
        if which == 1:
            loads[1].wait()
            pooled_ref[...] = jnp.transpose(pooled_raw[...], (1, 0, 2))
        src, dst = (dproj_ref, dproj_all) if which == 0 else (pooled_ref, pooled_all)
        copies = []
        for k in range(1, n_tab):
            to = lax.rem(tab + k, n_tab)
            copy = remote(
                columns(src, to, which), columns(dst, tab, which),
                a_send.at[which, k], a_recv.at[which, k], to, rep,
            )
            copy.start()
            copies.append(copy)
        gathers.append(copies)
    own = [
        pltpu.make_async_copy(src.at[tab], dst.at[tab], own_sem.at[which])
        for which, (src, dst) in enumerate(((dproj_ref, dproj_all), (pooled_ref, pooled_all)))
    ]
    for copy in own:
        copy.start()

    for copy in loads[2:4]:
        copy.wait()
    named = rows_ref[...]
    slots = lax.broadcasted_iota(jnp.int32, named.shape, 0)
    named = jnp.where(slots < lens_ref[...], named, -1)
    step = 64

    def count(i, carry):
        at = pl.multiple_of(i * step, step)
        ids = lax.broadcasted_iota(jnp.int32, (step, named.shape[1]), 0) + at
        total = jnp.zeros((step, named.shape[1]), F32)
        for slot in range(named.shape[0]):
            total = total + jnp.where(named[slot : slot + 1, :] == ids, 1.0, 0.0)
        counts[pl.ds(at, step), :] = total.astype(BF16)
        return carry

    lax.fori_loop(0, counts.shape[0] // step, count, 0)

    buffers = [
        (row_own, row_wire, row_sum),
        (proj_own.at[0], proj_wire.at[0], proj_sum.at[0]),
        (proj_own.at[1], proj_wire.at[1], proj_sum.at[1]),
    ]

    def send_pair(which):
        sums, wire, _ = buffers[which]
        wire[0] = sums[1 - y].astype(BF16)
        copy = remote(wire.at[0], wire.at[1], y_send.at[which], y_recv.at[which], tab, partner)
        copy.start()
        return copy

    def send_line(which, pair):
        sums, wire, _ = buffers[which]
        pair.wait_recv()
        total = sums[y] + wire[1].astype(F32)
        wire[2] = total.astype(BF16)
        copies = []
        for k in range(1, n_z):
            to = lax.rem(z + k, n_z)
            copy = remote(
                wire.at[2, to], wire.at[3, k], z_send.at[which, k], z_recv.at[which, k],
                tab, 2 * to + y,
            )
            copy.start()
            copies.append(copy)
        sums[y] = total
        return copies

    def send_sums(which, line):
        sums, wire, out = buffers[which]
        for copy in line:
            copy.wait_recv()
        total = sums[y, z]
        for k in range(1, n_z):
            total = total + wire[3, k].astype(F32)
        if which == 0:
            part = total.shape[0]
            coded, powers = encode(total)
            out[y, z, :part] = coded
            out[y, z, part:] = powers
        else:
            first = (which - 1) * piece + (y * n_z + z) * total.shape[0]
            at = lax.broadcasted_iota(jnp.int32, total.shape, 0) + first
            out[y, z] = jnp.where(at < limit, total, 0.0).astype(BF16)
        block = out.at[y, z]
        copies = []
        for k in range(1, n_z):
            copy = remote(
                block, block, g_send.at[which, 0, k], g_recv.at[which, 0, k],
                tab, 2 * lax.rem(z + k, n_z) + y,
            )
            copy.start()
            copies.append(copy)
        copy = remote(
            block, block, g_send.at[which, 1, 0], g_recv.at[which, 1, 0], tab, partner
        )
        copy.start()
        return copies, copy

    def forward(which, arriving):
        out = buffers[which][2]
        copies = []
        for k in range(1, n_z):
            arriving[k - 1].wait_recv()
            block = out.at[y, lax.rem(z - k + n_z, n_z)]
            copy = remote(
                block, block, g_send.at[which, 1, k], g_recv.at[which, 1, k], tab, partner
            )
            copy.start()
            copies.append(copy)
        return copies

    def project(half):
        total = None
        for k in range(n_tab):
            if k > 0:
                gathers[1 + half][k - 1].wait_recv()
            at = lax.rem(tab - k + n_tab, n_tab)
            term = lax.dot_general(
                pooled_all[at, :, half * piece : (half + 1) * piece], dproj_all[at],
                (((0,), (0,)), ((), ())), preferred_element_type=F32,
            )
            total = term if total is None else total + term
        proj_own[half] = total.reshape(proj_own.shape[1:])
        return send_pair(1 + half)

    for copy in loads[4:]:
        copy.wait()
    limit = weight_ref.shape[0] // 16 * dims_ref[tab]
    at_row = lax.broadcasted_iota(jnp.int32, weight_ref.shape, 0)
    live_weight[...] = jnp.where(at_row < limit, weight_ref[...].astype(F32), 0.0).astype(BF16)
    stores = [
        pltpu.make_async_copy(src, dst, store_sem.at[i])
        for i, (src, dst) in enumerate((
            (emb_buf.at[0], out_emb.at[y]),
            (emb_buf.at[1], out_emb.at[1 - y]),
            (proj_buf.at[0], out_proj.at[0]),
            (proj_buf.at[1], out_proj.at[1]),
        ))
    ]

    def table_rows(slot, half):
        part = row_sum.shape[2] - SCALE_ROWS
        total = jnp.concatenate(
            [decode(row_sum[half, i, :part], row_sum[half, i, part:]) for i in range(n_z)], axis=0
        )
        high = total.astype(BF16)
        low = (total - high.astype(F32)).astype(BF16)
        weight = live_weight[...]
        emb_buf[slot] = lax.dot_general(
            high, weight, (((1,), (1,)), ((), ())), preferred_element_type=F32
        ) + lax.dot_general(low, weight, (((1,), (1,)), ((), ())), preferred_element_type=F32)
        stores[slot].start()

    own[0].wait()
    for copy in gathers[0]:
        copy.wait_recv()
    d_all = dproj_all[...].reshape(n_tab * n_samples, width)
    row_own[...] = jnp.dot(counts[...], d_all, preferred_element_type=F32).reshape(row_own.shape)
    pair0 = send_pair(0)
    own[1].wait()
    pair1 = project(0)
    line0 = send_line(0, pair0)
    pair2 = project(1)
    line1 = send_line(1, pair1)
    line2 = send_line(2, pair2)
    sums0, last0 = send_sums(0, line0)
    sums1, last1 = send_sums(1, line1)
    sums2, last2 = send_sums(2, line2)
    fwd0 = forward(0, sums0)
    fwd1 = forward(1, sums1)
    fwd2 = forward(2, sums2)
    table_rows(0, y)
    for copy in [last0, *fwd0]:
        copy.wait_recv()
    table_rows(1, 1 - y)
    for half, copies in enumerate(([last1, *fwd1], [last2, *fwd2])):
        for copy in copies:
            copy.wait_recv()
        proj_buf[half] = proj_sum[half].astype(F32).reshape(proj_buf.shape[1:])
        stores[2 + half].start()
    for copy in [
        *gathers[0], *gathers[1], *gathers[2], pair0, pair1, pair2,
        *line0, *line1, *line2, *sums0, *sums1, *sums2,
        last0, last1, last2, *fwd0, *fwd1, *fwd2,
    ]:
        copy.wait_send()
    for copy in stores:
        copy.wait()


def finish(emb_from, proj_from, emb_to, proj_to, sem):
    copies = [
        pltpu.make_async_copy(src.at[i], dst.at[i], sem.at[which, i])
        for which, (src, dst) in enumerate(((proj_from, proj_to), (emb_from, emb_to)))
        for i in range(src.shape[0])
    ]
    for copy in copies:
        copy.start()
    for copy in copies:
        copy.wait()


def fused(n_tab, n_rep, d_proj, pooled, proj, bag_rows, bag_lengths, dim_blocks):
    n_samples, width, widest = d_proj.shape[1], d_proj.shape[3], pooled.shape[3]
    group, bag = bag_rows.shape[1], bag_rows.shape[3]
    n_z = n_rep // 2
    part, proj_part = ROWS // n_rep, widest // 2 // n_rep
    hbm = pl.BlockSpec(memory_space=pltpu.HBM)
    dma = pltpu.SemaphoreType.DMA
    emb, proj_grad = pl.pallas_call(
        functools.partial(kernel, n_tab, n_rep),
        out_shape=(
            jax.ShapeDtypeStruct((2, ROWS // 2, widest), F32),
            jax.ShapeDtypeStruct((2, widest // 2, width), F32),
        ),
        in_specs=[hbm] * 6,
        out_specs=(hbm, hbm),
        scratch_shapes=[
            pltpu.VMEM((2, n_z, part + SCALE_ROWS, width), jnp.int16),
            pltpu.VMEM((2, 2, n_z, proj_part, width), BF16),
            pltpu.VMEM((2, ROWS // 2, widest), F32),
            pltpu.VMEM((2, widest // 2, width), F32),
            pltpu.VMEM((widest, width), BF16),
            pltpu.VMEM((n_samples, n_tab, width), BF16),
            pltpu.VMEM((n_samples, n_tab, widest), BF16),
            pltpu.VMEM((n_tab, n_samples, width), BF16),
            pltpu.VMEM((n_tab, n_samples, widest), BF16),
            pltpu.VMEM((bag, group), jnp.int32),
            pltpu.VMEM((1, group), jnp.int32),
            pltpu.VMEM((widest, width), BF16),
            pltpu.SMEM((n_tab,), jnp.int32),
            pltpu.VMEM((n_tab, n_samples, width), BF16),
            pltpu.VMEM((n_tab, n_samples, widest), BF16),
            pltpu.VMEM((ROWS, group), BF16),
            pltpu.VMEM((2, n_z, part, width), F32),
            pltpu.VMEM((4, n_z, part, width), BF16),
            pltpu.VMEM((2, 2, n_z, proj_part, width), F32),
            pltpu.VMEM((2, 4, n_z, proj_part, width), BF16),
            dma((6,)),
            dma((4,)),
            dma((2,)),
            dma((3, n_tab)),
            dma((3, n_tab)),
            dma((3,)),
            dma((3,)),
            dma((3, n_z)),
            dma((3, n_z)),
            dma((3, 2, n_z)),
            dma((3, 2, n_z)),
        ],
        compiler_params=pltpu.CompilerParams(
            collective_id=0, has_side_effects=True, vmem_limit_bytes=60 << 20
        ),
    )(
        d_proj[0],
        pooled[0],
        jnp.transpose(bag_rows[0, :, 0, :]),
        bag_lengths.reshape(1, group),
        proj,
        dim_blocks,
    )
    emb, proj_grad = pl.pallas_call(
        finish,
        out_shape=(
            jax.ShapeDtypeStruct(emb.shape, F32),
            jax.ShapeDtypeStruct(proj_grad.shape, F32),
        ),
        in_specs=[hbm] * 2,
        out_specs=(hbm, hbm),
        scratch_shapes=[dma((2, 2))],
        compiler_params=pltpu.CompilerParams(vmem_limit_bytes=60 << 20),
        cost_estimate=pl.CostEstimate(
            flops=0, bytes_accessed=8 * (ROWS + width) * widest, transcendentals=0
        ),
    )(emb, proj_grad)
    return emb.reshape(1, ROWS, widest), proj_grad.reshape(1, widest, width)


def general(d_proj, pooled, proj, bag_rows, bag_lengths, dim_blocks):
    widest = proj.shape[1]
    group_rows = bag_rows.shape[1]
    bag_size = bag_rows.shape[3]
    columns = jnp.arange(widest, dtype=jnp.int32)
    live = (columns[None, :] < (widest // 16 * dim_blocks)[:, None]).astype(F32)
    samples_proj = d_proj[0]
    masked_pool = jnp.where(live[None, :, :] > 0, pooled[0], jnp.zeros_like(pooled[0]))
    proj_part = lax.psum_scatter(
        jnp.einsum("bte,btp->tep", masked_pool, samples_proj, preferred_element_type=F32),
        "tab",
        scatter_dimension=0,
        tiled=True,
    )
    back = jnp.einsum("btp,tep->bte", samples_proj, proj, preferred_element_type=F32)
    back = (back * live[None, :, :]).astype(BF16)
    d_pooled = lax.all_to_all(back, "tab", split_axis=1, concat_axis=0, tiled=True)
    row_ids = jnp.arange(ROWS, dtype=jnp.int32)
    counts = jnp.zeros((group_rows, ROWS), F32)
    for slot in range(bag_size):
        hit = (bag_rows[0, :, 0, slot][:, None] == row_ids[None, :]) & (
            slot < bag_lengths[0, :, 0]
        )[:, None]
        counts = counts + hit.astype(F32)
    emb_part = lax.dot_general(
        counts.astype(BF16), d_pooled[:, 0, :], (((0,), (0,)), ((), ())),
        preferred_element_type=F32,
    )
    return lax.psum((emb_part[None], proj_part), "rep")


def solution(mesh):
    n_tab, n_rep = mesh.shape["tab"], mesh.shape["rep"]
    placed = (
        P("rep", "tab", None, None),
        P("rep", "tab", None, None),
        P(),
        P("rep", None, "tab", None),
        P("rep", None, "tab"),
        P(),
    )

    def body(*args):
        if n_rep % 2 == 0 and ROWS % (16 * n_rep) == 0 and args[2].shape[1] % (32 * n_rep) == 0:
            return fused(n_tab, n_rep, *args)
        return general(*args)

    return jax.shard_map(
        body,
        mesh=mesh,
        in_specs=placed,
        out_specs=(P("tab", None, None), P("tab", None, None)),
        check_vma=False,
    )
```

```python
import functools

import jax
import jax.numpy as jnp
from jax import lax
from jax.experimental import pallas as pl
from jax.experimental.pallas import tpu as pltpu
from jax.sharding import PartitionSpec as P

ROWS = 512
MESH = pl.DeviceIdType.MESH
BF16 = jnp.bfloat16
F32 = jnp.float32


SCALE_ROWS = 16


def encode(total):
    peak = jnp.maximum(jnp.max(jnp.abs(total), axis=0, keepdims=True), 1e-30)
    power = jnp.floor(jnp.log2(peak) + 1.01) - 15.0
    coded = jnp.floor(total * jnp.exp2(-power) + 0.5)
    coded = jnp.clip(coded, -32767.0, 32767.0).astype(jnp.int32).astype(jnp.int16)
    powers = jnp.broadcast_to(power, (SCALE_ROWS, total.shape[1]))
    return coded, powers.astype(jnp.int32).astype(jnp.int16)


def decode(coded, powers):
    scale = jnp.exp2(powers.astype(jnp.int32).astype(F32)[:1])
    return coded.astype(jnp.int32).astype(F32) * scale


def kernel(
    n_tab,
    n_rep,
    dproj_hbm,
    pooled_hbm,
    rows_hbm,
    lens_hbm,
    weight_hbm,
    dims_hbm,
    out_emb,
    out_proj,
    row_sum,
    proj_sum,
    emb_buf,
    proj_buf,
    live_weight,
    dproj_raw,
    pooled_raw,
    dproj_ref,
    pooled_ref,
    rows_ref,
    lens_ref,
    weight_ref,
    dims_ref,
    dproj_all,
    pooled_all,
    counts,
    row_own,
    row_wire,
    proj_own,
    proj_wire,
    load_sem,
    store_sem,
    own_sem,
    a_send,
    a_recv,
    y_send,
    y_recv,
    z_send,
    z_recv,
    g_send,
    g_recv,
):
    tab = lax.axis_index("tab")
    rep = lax.axis_index("rep")
    n_z = n_rep // 2
    y = lax.rem(rep, 2)
    z = rep // 2
    partner = rep + 1 - 2 * y
    n_samples, width = dproj_ref.shape[1], dproj_ref.shape[2]
    piece = pooled_ref.shape[1] // 2

    loads = [
        pltpu.make_async_copy(src, dst, load_sem.at[i])
        for i, (src, dst) in enumerate((
            (dproj_hbm, dproj_raw),
            (pooled_hbm, pooled_raw),
            (rows_hbm, rows_ref),
            (lens_hbm, lens_ref),
            (weight_hbm.at[tab], weight_ref),
            (dims_hbm, dims_ref),
        ))
    ]
    for copy in loads:
        copy.start()

    def remote(src, dst, send, recv, tab_to, rep_to):
        return pltpu.make_async_remote_copy(
            src_ref=src,
            dst_ref=dst,
            send_sem=send,
            recv_sem=recv,
            device_id=(tab_to, rep_to),
            device_id_type=MESH,
        )

    barrier = pltpu.get_barrier_semaphore()
    for k in range(1, n_tab):
        pl.semaphore_signal(
            barrier, inc=1, device_id=(lax.rem(tab + k, n_tab), rep), device_id_type=MESH
        )
    for k in range(1, n_z):
        pl.semaphore_signal(
            barrier, inc=1, device_id=(tab, lax.rem(rep + 2 * k, n_rep)), device_id_type=MESH
        )
    pl.semaphore_signal(barrier, inc=1, device_id=(tab, partner), device_id_type=MESH)
    loads[0].wait()
    dproj_ref[...] = jnp.transpose(dproj_raw[...], (1, 0, 2))
    pl.semaphore_wait(barrier, n_tab - 1 + n_z)

    def columns(ref, at, which):
        return ref.at[at] if which == 0 else ref.at[at, pl.ds((which - 1) * piece, piece)]

    gathers = []
    for which in range(3):
        if which == 1:
            loads[1].wait()
            by_table = jnp.transpose(pooled_raw[...], (1, 0, 2))
        if which > 0:
            at = (which - 1) * piece
            for table in range(n_tab):
                pooled_ref[table, at : at + piece] = by_table[table, :, at : at + piece].T
        src, dst = (dproj_ref, dproj_all) if which == 0 else (pooled_ref, pooled_all)
        copies = []
        for k in range(1, n_tab):
            to = lax.rem(tab + k, n_tab)
            copy = remote(
                columns(src, to, which), columns(dst, tab, which),
                a_send.at[which, k], a_recv.at[which, k], to, rep,
            )
            copy.start()
            copies.append(copy)
        gathers.append(copies)
    own = pltpu.make_async_copy(dproj_ref.at[tab], dproj_all.at[tab], own_sem.at[0])
    own.start()

    for copy in loads[2:4]:
        copy.wait()
    named = rows_ref[...]
    slots = lax.broadcasted_iota(jnp.int32, named.shape, 0)
    named = jnp.where(slots < lens_ref[...], named, -1)
    step = 64

    def count(i, carry):
        at = pl.multiple_of(i * step, step)
        ids = lax.broadcasted_iota(jnp.int32, (step, named.shape[1]), 0) + at
        total = jnp.zeros((step, named.shape[1]), F32)
        for slot in range(named.shape[0]):
            total = total + jnp.where(named[slot : slot + 1, :] == ids, 1.0, 0.0)
        counts[pl.ds(at, step), :] = total.astype(BF16)
        return carry

    lax.fori_loop(0, counts.shape[0] // step, count, 0)

    buffers = [
        (row_own, row_wire, row_sum),
        (proj_own.at[0], proj_wire.at[0], proj_sum.at[0]),
        (proj_own.at[1], proj_wire.at[1], proj_sum.at[1]),
    ]

    def send_pair(which):
        sums, wire, _ = buffers[which]
        wire[0] = sums[1 - y].astype(BF16)
        copy = remote(wire.at[0], wire.at[1], y_send.at[which], y_recv.at[which], tab, partner)
        copy.start()
        return copy

    def send_line(which, pair):
        sums, wire, _ = buffers[which]
        pair.wait_recv()
        total = sums[y] + wire[1].astype(F32)
        wire[2] = total.astype(BF16)
        copies = []
        for k in range(1, n_z):
            to = lax.rem(z + k, n_z)
            copy = remote(
                wire.at[2, to], wire.at[3, k], z_send.at[which, k], z_recv.at[which, k],
                tab, 2 * to + y,
            )
            copy.start()
            copies.append(copy)
        sums[y] = total
        return copies

    def send_sums(which, line):
        sums, wire, out = buffers[which]
        for copy in line:
            copy.wait_recv()
        total = sums[y, z]
        for k in range(1, n_z):
            total = total + wire[3, k].astype(F32)
        if which == 0:
            part = total.shape[0]
            coded, powers = encode(total)
            out[y, z, :part] = coded
            out[y, z, part:] = powers
        else:
            first = (which - 1) * piece + (y * n_z + z) * total.shape[0]
            at = lax.broadcasted_iota(jnp.int32, total.shape, 0) + first
            out[y, z] = jnp.where(at < limit, total, 0.0).astype(BF16)
        block = out.at[y, z]
        copies = []
        for k in range(1, n_z):
            copy = remote(
                block, block, g_send.at[which, 0, k], g_recv.at[which, 0, k],
                tab, 2 * lax.rem(z + k, n_z) + y,
            )
            copy.start()
            copies.append(copy)
        copy = remote(
            block, block, g_send.at[which, 1, 0], g_recv.at[which, 1, 0], tab, partner
        )
        copy.start()
        return copies, copy

    def forward(which, arriving):
        out = buffers[which][2]
        copies = []
        for k in range(1, n_z):
            arriving[k - 1].wait_recv()
            block = out.at[y, lax.rem(z - k + n_z, n_z)]
            copy = remote(
                block, block, g_send.at[which, 1, k], g_recv.at[which, 1, k], tab, partner
            )
            copy.start()
            copies.append(copy)
        return copies

    def project(half):
        total = None
        for k in range(n_tab):
            if k > 0:
                gathers[1 + half][k - 1].wait_recv()
            at = lax.rem(tab - k + n_tab, n_tab)
            block = (pooled_all if k > 0 else pooled_ref)[at, half * piece : (half + 1) * piece]
            term = jnp.dot(block, dproj_all[at], preferred_element_type=F32)
            total = term if total is None else total + term
        proj_own[half] = total.reshape(proj_own.shape[1:])
        return send_pair(1 + half)

    for copy in loads[4:]:
        copy.wait()
    limit = weight_ref.shape[0] // 16 * dims_ref[tab]
    at_row = lax.broadcasted_iota(jnp.int32, weight_ref.shape, 0)
    live_weight[...] = jnp.where(at_row < limit, weight_ref[...].astype(F32), 0.0).astype(BF16)
    stores = [
        pltpu.make_async_copy(src, dst, store_sem.at[i])
        for i, (src, dst) in enumerate((
            (emb_buf.at[0], out_emb.at[y]),
            (emb_buf.at[1], out_emb.at[1 - y]),
            (proj_buf.at[0], out_proj.at[0]),
            (proj_buf.at[1], out_proj.at[1]),
        ))
    ]

    def table_rows(slot, half):
        part = row_sum.shape[2] - SCALE_ROWS
        total = jnp.concatenate(
            [decode(row_sum[half, i, :part], row_sum[half, i, part:]) for i in range(n_z)], axis=0
        )
        high = total.astype(BF16)
        low = (total - high.astype(F32)).astype(BF16)
        weight = live_weight[...]
        emb_buf[slot] = lax.dot_general(
            high, weight, (((1,), (1,)), ((), ())), preferred_element_type=F32
        ) + lax.dot_general(low, weight, (((1,), (1,)), ((), ())), preferred_element_type=F32)
        stores[slot].start()

    own.wait()
    for copy in gathers[0]:
        copy.wait_recv()
    d_all = dproj_all[...].reshape(n_tab * n_samples, width)
    row_own[...] = jnp.dot(counts[...], d_all, preferred_element_type=F32).reshape(row_own.shape)
    pair0 = send_pair(0)
    pair1 = project(0)
    line0 = send_line(0, pair0)
    pair2 = project(1)
    line1 = send_line(1, pair1)
    line2 = send_line(2, pair2)
    sums0, last0 = send_sums(0, line0)
    sums1, last1 = send_sums(1, line1)
    sums2, last2 = send_sums(2, line2)
    fwd0 = forward(0, sums0)
    fwd1 = forward(1, sums1)
    fwd2 = forward(2, sums2)
    table_rows(0, y)
    for copy in [last0, *fwd0]:
        copy.wait_recv()
    table_rows(1, 1 - y)
    for half, copies in enumerate(([last1, *fwd1], [last2, *fwd2])):
        for copy in copies:
            copy.wait_recv()
        proj_buf[half] = proj_sum[half].astype(F32).reshape(proj_buf.shape[1:])
        stores[2 + half].start()
    for copy in [
        *gathers[0], *gathers[1], *gathers[2], pair0, pair1, pair2,
        *line0, *line1, *line2, *sums0, *sums1, *sums2,
        last0, last1, last2, *fwd0, *fwd1, *fwd2,
    ]:
        copy.wait_send()
    for copy in stores:
        copy.wait()


def finish(emb_from, proj_from, emb_to, proj_to, emb_buf, proj_buf, load_sem, store_sem):
    loads, stores = [], []
    for which, (src, buf, dst) in enumerate(
        ((proj_from, proj_buf, proj_to), (emb_from, emb_buf, emb_to))
    ):
        for i in range(src.shape[0]):
            loads.append(pltpu.make_async_copy(src.at[i], buf.at[i], load_sem.at[which, i]))
            stores.append(pltpu.make_async_copy(buf.at[i], dst.at[i], store_sem.at[which, i]))
    for copy in loads:
        copy.start()
    for load, copy in zip(loads, stores):
        load.wait()
        copy.start()
    for copy in stores:
        copy.wait()


def fused(n_tab, n_rep, d_proj, pooled, proj, bag_rows, bag_lengths, dim_blocks):
    n_samples, width, widest = d_proj.shape[1], d_proj.shape[3], pooled.shape[3]
    group, bag = bag_rows.shape[1], bag_rows.shape[3]
    n_z = n_rep // 2
    part, proj_part = ROWS // n_rep, widest // 2 // n_rep
    hbm = pl.BlockSpec(memory_space=pltpu.HBM)
    dma = pltpu.SemaphoreType.DMA
    emb, proj_grad = pl.pallas_call(
        functools.partial(kernel, n_tab, n_rep),
        out_shape=(
            jax.ShapeDtypeStruct((2, ROWS // 2, widest), F32),
            jax.ShapeDtypeStruct((2, widest // 2, width), F32),
        ),
        in_specs=[hbm] * 6,
        out_specs=(hbm, hbm),
        scratch_shapes=[
            pltpu.VMEM((2, n_z, part + SCALE_ROWS, width), jnp.int16),
            pltpu.VMEM((2, 2, n_z, proj_part, width), BF16),
            pltpu.VMEM((2, ROWS // 2, widest), F32),
            pltpu.VMEM((2, widest // 2, width), F32),
            pltpu.VMEM((widest, width), BF16),
            pltpu.VMEM((n_samples, n_tab, width), BF16),
            pltpu.VMEM((n_samples, n_tab, widest), BF16),
            pltpu.VMEM((n_tab, n_samples, width), BF16),
            pltpu.VMEM((n_tab, widest, n_samples), BF16),
            pltpu.VMEM((bag, group), jnp.int32),
            pltpu.VMEM((1, group), jnp.int32),
            pltpu.VMEM((widest, width), BF16),
            pltpu.SMEM((n_tab,), jnp.int32),
            pltpu.VMEM((n_tab, n_samples, width), BF16),
            pltpu.VMEM((n_tab, widest, n_samples), BF16),
            pltpu.VMEM((ROWS, group), BF16),
            pltpu.VMEM((2, n_z, part, width), F32),
            pltpu.VMEM((4, n_z, part, width), BF16),
            pltpu.VMEM((2, 2, n_z, proj_part, width), F32),
            pltpu.VMEM((2, 4, n_z, proj_part, width), BF16),
            dma((6,)),
            dma((4,)),
            dma((1,)),
            dma((3, n_tab)),
            dma((3, n_tab)),
            dma((3,)),
            dma((3,)),
            dma((3, n_z)),
            dma((3, n_z)),
            dma((3, 2, n_z)),
            dma((3, 2, n_z)),
        ],
        compiler_params=pltpu.CompilerParams(
            collective_id=0, has_side_effects=True, vmem_limit_bytes=60 << 20
        ),
    )(
        d_proj[0],
        pooled[0],
        jnp.transpose(bag_rows[0, :, 0, :]),
        bag_lengths.reshape(1, group),
        proj,
        dim_blocks,
    )
    tiles = 4
    emb = emb.reshape(tiles, ROWS // tiles, widest)
    proj_grad = proj_grad.reshape(tiles, widest // tiles, width)
    emb, proj_grad = pl.pallas_call(
        finish,
        out_shape=(
            jax.ShapeDtypeStruct(emb.shape, F32),
            jax.ShapeDtypeStruct(proj_grad.shape, F32),
        ),
        in_specs=[hbm] * 2,
        out_specs=(hbm, hbm),
        scratch_shapes=[
            pltpu.VMEM(emb.shape, F32),
            pltpu.VMEM(proj_grad.shape, F32),
            dma((2, tiles)),
            dma((2, tiles)),
        ],
        compiler_params=pltpu.CompilerParams(vmem_limit_bytes=60 << 20),
        cost_estimate=pl.CostEstimate(
            flops=0, bytes_accessed=8 * (ROWS + width) * widest, transcendentals=0
        ),
    )(emb, proj_grad)
    return emb.reshape(1, ROWS, widest), proj_grad.reshape(1, widest, width)


def general(d_proj, pooled, proj, bag_rows, bag_lengths, dim_blocks):
    widest = proj.shape[1]
    group_rows = bag_rows.shape[1]
    bag_size = bag_rows.shape[3]
    columns = jnp.arange(widest, dtype=jnp.int32)
    live = (columns[None, :] < (widest // 16 * dim_blocks)[:, None]).astype(F32)
    samples_proj = d_proj[0]
    masked_pool = jnp.where(live[None, :, :] > 0, pooled[0], jnp.zeros_like(pooled[0]))
    proj_part = lax.psum_scatter(
        jnp.einsum("bte,btp->tep", masked_pool, samples_proj, preferred_element_type=F32),
        "tab",
        scatter_dimension=0,
        tiled=True,
    )
    back = jnp.einsum("btp,tep->bte", samples_proj, proj, preferred_element_type=F32)
    back = (back * live[None, :, :]).astype(BF16)
    d_pooled = lax.all_to_all(back, "tab", split_axis=1, concat_axis=0, tiled=True)
    row_ids = jnp.arange(ROWS, dtype=jnp.int32)
    counts = jnp.zeros((group_rows, ROWS), F32)
    for slot in range(bag_size):
        hit = (bag_rows[0, :, 0, slot][:, None] == row_ids[None, :]) & (
            slot < bag_lengths[0, :, 0]
        )[:, None]
        counts = counts + hit.astype(F32)
    emb_part = lax.dot_general(
        counts.astype(BF16), d_pooled[:, 0, :], (((0,), (0,)), ((), ())),
        preferred_element_type=F32,
    )
    return lax.psum((emb_part[None], proj_part), "rep")


def solution(mesh):
    n_tab, n_rep = mesh.shape["tab"], mesh.shape["rep"]
    placed = (
        P("rep", "tab", None, None),
        P("rep", "tab", None, None),
        P(),
        P("rep", None, "tab", None),
        P("rep", None, "tab"),
        P(),
    )

    def body(*args):
        if n_rep % 2 == 0 and ROWS % (16 * n_rep) == 0 and args[2].shape[1] % (32 * n_rep) == 0:
            return fused(n_tab, n_rep, *args)
        return general(*args)

    return jax.shard_map(
        body,
        mesh=mesh,
        in_specs=placed,
        out_specs=(P("tab", None, None), P("tab", None, None)),
        check_vma=False,
    )
```

```python
import functools

import jax
import jax.numpy as jnp
from jax import lax
from jax.experimental import pallas as pl
from jax.experimental.pallas import tpu as pltpu
from jax.sharding import PartitionSpec as P

ROWS = 512
MESH = pl.DeviceIdType.MESH
BF16 = jnp.bfloat16
F32 = jnp.float32


SCALE_ROWS = 16


def encode(total):
    peak = jnp.maximum(jnp.max(jnp.abs(total), axis=0, keepdims=True), 1e-30)
    power = jnp.floor(jnp.log2(peak) + 1.01) - 15.0
    coded = jnp.floor(total * jnp.exp2(-power) + 0.5)
    coded = jnp.clip(coded, -32767.0, 32767.0).astype(jnp.int32).astype(jnp.int16)
    powers = jnp.broadcast_to(power, (SCALE_ROWS, total.shape[1]))
    return coded, powers.astype(jnp.int32).astype(jnp.int16)


def decode(coded, powers):
    scale = jnp.exp2(powers.astype(jnp.int32).astype(F32)[:1])
    return coded.astype(jnp.int32).astype(F32) * scale


def kernel(
    n_tab,
    n_rep,
    dproj_hbm,
    pooled_hbm,
    rows_hbm,
    lens_hbm,
    weight_hbm,
    dims_hbm,
    out_emb,
    out_proj,
    row_sum,
    proj_sum,
    emb_buf,
    live_weight,
    dproj_raw,
    pooled_raw,
    dproj_ref,
    pooled_ref,
    rows_ref,
    lens_ref,
    weight_ref,
    dims_ref,
    dproj_all,
    pooled_all,
    counts,
    row_own,
    row_wire,
    proj_own,
    proj_wire,
    load_sem,
    store_sem,
    own_sem,
    a_send,
    a_recv,
    c_send,
    c_recv,
    y_send,
    y_recv,
    z_send,
    z_recv,
    g_send,
    g_recv,
):
    tab = lax.axis_index("tab")
    rep = lax.axis_index("rep")
    n_z = n_rep // 2
    y = lax.rem(rep, 2)
    z = rep // 2
    partner = rep + 1 - 2 * y
    n_samples, width = dproj_ref.shape[1], dproj_ref.shape[2]
    piece = pooled_ref.shape[1] // 2

    loads = [
        pltpu.make_async_copy(src, dst, load_sem.at[i])
        for i, (src, dst) in enumerate((
            (dproj_hbm, dproj_raw),
            (pooled_hbm, pooled_raw),
            (rows_hbm, rows_ref),
            (lens_hbm, lens_ref),
            (weight_hbm.at[tab], weight_ref),
            (dims_hbm, dims_ref),
        ))
    ]
    for copy in loads:
        copy.start()

    def remote(src, dst, send, recv, tab_to, rep_to):
        return pltpu.make_async_remote_copy(
            src_ref=src,
            dst_ref=dst,
            send_sem=send,
            recv_sem=recv,
            device_id=(tab_to, rep_to),
            device_id_type=MESH,
        )

    barrier = pltpu.get_barrier_semaphore()
    for k in range(1, n_tab):
        pl.semaphore_signal(
            barrier, inc=1, device_id=(lax.rem(tab + k, n_tab), rep), device_id_type=MESH
        )
    for k in range(1, n_rep):
        pl.semaphore_signal(
            barrier, inc=1, device_id=(tab, lax.rem(rep + k, n_rep)), device_id_type=MESH
        )
    loads[0].wait()
    dproj_ref[...] = jnp.transpose(dproj_raw[...], (1, 0, 2))
    pl.semaphore_wait(barrier, n_tab + n_rep - 2)

    def columns(ref, at, which):
        return ref.at[at] if which == 0 else ref.at[at, pl.ds((which - 1) * piece, piece)]

    gathers = []
    for which in range(3):
        if which == 1:
            loads[1].wait()
            by_table = jnp.transpose(pooled_raw[...], (1, 0, 2))
        if which > 0:
            at = (which - 1) * piece
            for table in range(n_tab):
                pooled_ref[table, at : at + piece] = by_table[table, :, at : at + piece].T
        src, dst = (dproj_ref, dproj_all) if which == 0 else (pooled_ref, pooled_all)
        copies = []
        for k in range(1, n_tab):
            to = lax.rem(tab + k, n_tab)
            copy = remote(
                columns(src, to, which), columns(dst, tab, which),
                a_send.at[which, k], a_recv.at[which, k], to, rep,
            )
            copy.start()
            copies.append(copy)
        gathers.append(copies)
    own = pltpu.make_async_copy(dproj_ref.at[tab], dproj_all.at[tab], own_sem.at[0])
    own.start()

    for copy in loads[2:4]:
        copy.wait()
    named = rows_ref[...]
    slots = lax.broadcasted_iota(jnp.int32, named.shape, 0)
    named = jnp.where(slots < lens_ref[...], named, -1)
    step = 64

    def count(i, carry):
        at = pl.multiple_of(i * step, step)
        ids = lax.broadcasted_iota(jnp.int32, (step, named.shape[1]), 0) + at
        total = jnp.zeros((step, named.shape[1]), F32)
        for slot in range(named.shape[0]):
            total = total + jnp.where(named[slot : slot + 1, :] == ids, 1.0, 0.0)
        counts[pl.ds(at, step), :] = total.astype(BF16)
        return carry

    lax.fori_loop(0, counts.shape[0] // step, count, 0)

    buffers = [
        (row_own, row_wire, row_sum),
        (proj_own.at[0], proj_wire.at[0], proj_sum.at[0]),
        (proj_own.at[1], proj_wire.at[1], proj_sum.at[1]),
    ]

    def send_all():
        row_wire[0] = row_own[...].reshape(row_wire.shape[1:]).astype(BF16)
        copies = []
        for k in range(1, n_rep):
            to = lax.rem(rep + k, n_rep)
            slot = lax.rem(to, 2) * n_z + to // 2
            copy = remote(
                row_wire.at[0, slot], row_wire.at[1, k], c_send.at[k], c_recv.at[k], tab, to
            )
            copy.start()
            copies.append(copy)
        return copies

    def send_pair(which):
        sums, wire, _ = buffers[which]
        wire[0] = sums[1 - y].astype(BF16)
        copy = remote(wire.at[0], wire.at[1], y_send.at[which], y_recv.at[which], tab, partner)
        copy.start()
        return copy

    def send_line(which, pair):
        sums, wire, _ = buffers[which]
        pair.wait_recv()
        total = sums[y] + wire[1].astype(F32)
        wire[2] = total.astype(BF16)
        copies = []
        for k in range(1, n_z):
            to = lax.rem(z + k, n_z)
            copy = remote(
                wire.at[2, to], wire.at[3, k], z_send.at[which, k], z_recv.at[which, k],
                tab, 2 * to + y,
            )
            copy.start()
            copies.append(copy)
        sums[y] = total
        return copies

    def send_sums(which, line):
        sums, wire, out = buffers[which]
        for copy in line:
            copy.wait_recv()
        total = sums[y, z]
        for k in range(1, n_rep if which == 0 else n_z):
            total = total + (wire[1, k] if which == 0 else wire[3, k]).astype(F32)
        if which == 0:
            part = total.shape[0]
            coded, powers = encode(total)
            out[y, z, :part] = coded
            out[y, z, part:] = powers
        else:
            first = (which - 1) * piece + (y * n_z + z) * total.shape[0]
            at = lax.broadcasted_iota(jnp.int32, total.shape, 0) + first
            out[y, z] = jnp.where(at < limit, total, 0.0).astype(BF16)
        block = out.at[y, z]
        copies = []
        for k in range(1, n_z):
            copy = remote(
                block, block, g_send.at[which, 0, k], g_recv.at[which, 0, k],
                tab, 2 * lax.rem(z + k, n_z) + y,
            )
            copy.start()
            copies.append(copy)
        copy = remote(
            block, block, g_send.at[which, 1, 0], g_recv.at[which, 1, 0], tab, partner
        )
        copy.start()
        return copies, copy

    def forward(which, arriving):
        out = buffers[which][2]
        copies = []
        for k in range(1, n_z):
            arriving[k - 1].wait_recv()
            block = out.at[y, lax.rem(z - k + n_z, n_z)]
            copy = remote(
                block, block, g_send.at[which, 1, k], g_recv.at[which, 1, k], tab, partner
            )
            copy.start()
            copies.append(copy)
        return copies

    def project(half):
        total = None
        for k in range(n_tab):
            if k > 0:
                gathers[1 + half][k - 1].wait_recv()
            at = lax.rem(tab - k + n_tab, n_tab)
            block = (pooled_all if k > 0 else pooled_ref)[at, half * piece : (half + 1) * piece]
            term = jnp.dot(block, dproj_all[at], preferred_element_type=F32)
            total = term if total is None else total + term
        proj_own[half] = total.reshape(proj_own.shape[1:])
        return send_pair(1 + half)

    for copy in loads[4:]:
        copy.wait()
    limit = weight_ref.shape[0] // 16 * dims_ref[tab]
    at_row = lax.broadcasted_iota(jnp.int32, weight_ref.shape, 0)
    live_weight[...] = jnp.where(at_row < limit, weight_ref[...].astype(F32), 0.0).astype(BF16)
    stores = [
        pltpu.make_async_copy(src, dst, store_sem.at[i])
        for i, (src, dst) in enumerate((
            (emb_buf.at[0], out_emb.at[y]),
            (emb_buf.at[1], out_emb.at[1 - y]),
            (proj_sum.at[0], out_proj.at[0]),
            (proj_sum.at[1], out_proj.at[1]),
        ))
    ]

    def table_rows(slot, half):
        part = row_sum.shape[2] - SCALE_ROWS
        total = jnp.concatenate(
            [decode(row_sum[half, i, :part], row_sum[half, i, part:]) for i in range(n_z)], axis=0
        )
        high = total.astype(BF16)
        low = (total - high.astype(F32)).astype(BF16)
        weight = live_weight[...]
        emb_buf[slot] = lax.dot_general(
            high, weight, (((1,), (1,)), ((), ())), preferred_element_type=F32
        ) + lax.dot_general(low, weight, (((1,), (1,)), ((), ())), preferred_element_type=F32)
        stores[slot].start()

    own.wait()
    for copy in gathers[0]:
        copy.wait_recv()
    d_all = dproj_all[...].reshape(n_tab * n_samples, width)
    row_own[...] = jnp.dot(counts[...], d_all, preferred_element_type=F32).reshape(row_own.shape)
    line0 = send_all()
    pair1 = project(0)
    pair2 = project(1)
    line1 = send_line(1, pair1)
    line2 = send_line(2, pair2)
    sums0, last0 = send_sums(0, line0)
    sums1, last1 = send_sums(1, line1)
    sums2, last2 = send_sums(2, line2)
    fwd0 = forward(0, sums0)
    fwd1 = forward(1, sums1)
    fwd2 = forward(2, sums2)
    table_rows(0, y)
    for copy in [last0, *fwd0]:
        copy.wait_recv()
    table_rows(1, 1 - y)
    for half, copies in enumerate(([last1, *fwd1], [last2, *fwd2])):
        for copy in copies:
            copy.wait_recv()
        stores[2 + half].start()
    for copy in [
        *gathers[0], *gathers[1], *gathers[2], pair1, pair2,
        *line0, *line1, *line2, *sums0, *sums1, *sums2,
        last0, last1, last2, *fwd0, *fwd1, *fwd2,
    ]:
        copy.wait_send()
    for copy in stores:
        copy.wait()


def finish(
    emb_from, proj_from, emb_to, proj_to, emb_buf, proj_in, proj_out, load_sem, store_sem
):
    tiles = emb_from.shape[0]
    loads = [pltpu.make_async_copy(proj_from, proj_in, load_sem.at[tiles])]
    stores = [pltpu.make_async_copy(proj_out, proj_to, store_sem.at[tiles])]
    for i in range(tiles):
        loads.append(pltpu.make_async_copy(emb_from.at[i], emb_buf.at[i], load_sem.at[i]))
        stores.append(pltpu.make_async_copy(emb_buf.at[i], emb_to.at[i], store_sem.at[i]))
    for copy in loads:
        copy.start()
    for i in range(tiles + 1):
        loads[i].wait()
        if i == 0:
            proj_out[...] = proj_in[...].astype(F32)
        stores[i].start()
    for copy in stores:
        copy.wait()


def fused(n_tab, n_rep, d_proj, pooled, proj, bag_rows, bag_lengths, dim_blocks):
    n_samples, width, widest = d_proj.shape[1], d_proj.shape[3], pooled.shape[3]
    group, bag = bag_rows.shape[1], bag_rows.shape[3]
    n_z = n_rep // 2
    part, proj_part = ROWS // n_rep, widest // 2 // n_rep
    hbm = pl.BlockSpec(memory_space=pltpu.HBM)
    dma = pltpu.SemaphoreType.DMA
    emb, proj_grad = pl.pallas_call(
        functools.partial(kernel, n_tab, n_rep),
        out_shape=(
            jax.ShapeDtypeStruct((2, ROWS // 2, widest), F32),
            jax.ShapeDtypeStruct((2, 2, n_z, proj_part, width), BF16),
        ),
        in_specs=[hbm] * 6,
        out_specs=(hbm, hbm),
        scratch_shapes=[
            pltpu.VMEM((2, n_z, part + SCALE_ROWS, width), jnp.int16),
            pltpu.VMEM((2, 2, n_z, proj_part, width), BF16),
            pltpu.VMEM((2, ROWS // 2, widest), F32),
            pltpu.VMEM((widest, width), BF16),
            pltpu.VMEM((n_samples, n_tab, width), BF16),
            pltpu.VMEM((n_samples, n_tab, widest), BF16),
            pltpu.VMEM((n_tab, n_samples, width), BF16),
            pltpu.VMEM((n_tab, widest, n_samples), BF16),
            pltpu.VMEM((bag, group), jnp.int32),
            pltpu.VMEM((1, group), jnp.int32),
            pltpu.VMEM((widest, width), BF16),
            pltpu.SMEM((n_tab,), jnp.int32),
            pltpu.VMEM((n_tab, n_samples, width), BF16),
            pltpu.VMEM((n_tab, widest, n_samples), BF16),
            pltpu.VMEM((ROWS, group), BF16),
            pltpu.VMEM((2, n_z, part, width), F32),
            pltpu.VMEM((2, n_rep, part, width), BF16),
            pltpu.VMEM((2, 2, n_z, proj_part, width), F32),
            pltpu.VMEM((2, 4, n_z, proj_part, width), BF16),
            dma((6,)),
            dma((4,)),
            dma((1,)),
            dma((3, n_tab)),
            dma((3, n_tab)),
            dma((n_rep,)),
            dma((n_rep,)),
            dma((3,)),
            dma((3,)),
            dma((3, n_z)),
            dma((3, n_z)),
            dma((3, 2, n_z)),
            dma((3, 2, n_z)),
        ],
        compiler_params=pltpu.CompilerParams(
            collective_id=0, has_side_effects=True, vmem_limit_bytes=60 << 20
        ),
    )(
        d_proj[0],
        pooled[0],
        jnp.transpose(bag_rows[0, :, 0, :]),
        bag_lengths.reshape(1, group),
        proj,
        dim_blocks,
    )
    tiles = 4
    emb = emb.reshape(tiles, ROWS // tiles, widest)
    proj_grad = proj_grad.reshape(widest, width)
    emb, proj_grad = pl.pallas_call(
        finish,
        out_shape=(
            jax.ShapeDtypeStruct(emb.shape, F32),
            jax.ShapeDtypeStruct(proj_grad.shape, F32),
        ),
        in_specs=[hbm] * 2,
        out_specs=(hbm, hbm),
        scratch_shapes=[
            pltpu.VMEM(emb.shape, F32),
            pltpu.VMEM(proj_grad.shape, BF16),
            pltpu.VMEM(proj_grad.shape, F32),
            dma((tiles + 1,)),
            dma((tiles + 1,)),
        ],
        compiler_params=pltpu.CompilerParams(vmem_limit_bytes=60 << 20),
        cost_estimate=pl.CostEstimate(
            flops=0, bytes_accessed=8 * (ROWS + width) * widest, transcendentals=0
        ),
    )(emb, proj_grad)
    return emb.reshape(1, ROWS, widest), proj_grad.reshape(1, widest, width)


def general(d_proj, pooled, proj, bag_rows, bag_lengths, dim_blocks):
    widest = proj.shape[1]
    group_rows = bag_rows.shape[1]
    bag_size = bag_rows.shape[3]
    columns = jnp.arange(widest, dtype=jnp.int32)
    live = (columns[None, :] < (widest // 16 * dim_blocks)[:, None]).astype(F32)
    samples_proj = d_proj[0]
    masked_pool = jnp.where(live[None, :, :] > 0, pooled[0], jnp.zeros_like(pooled[0]))
    proj_part = lax.psum_scatter(
        jnp.einsum("bte,btp->tep", masked_pool, samples_proj, preferred_element_type=F32),
        "tab",
        scatter_dimension=0,
        tiled=True,
    )
    back = jnp.einsum("btp,tep->bte", samples_proj, proj, preferred_element_type=F32)
    back = (back * live[None, :, :]).astype(BF16)
    d_pooled = lax.all_to_all(back, "tab", split_axis=1, concat_axis=0, tiled=True)
    row_ids = jnp.arange(ROWS, dtype=jnp.int32)
    counts = jnp.zeros((group_rows, ROWS), F32)
    for slot in range(bag_size):
        hit = (bag_rows[0, :, 0, slot][:, None] == row_ids[None, :]) & (
            slot < bag_lengths[0, :, 0]
        )[:, None]
        counts = counts + hit.astype(F32)
    emb_part = lax.dot_general(
        counts.astype(BF16), d_pooled[:, 0, :], (((0,), (0,)), ((), ())),
        preferred_element_type=F32,
    )
    return lax.psum((emb_part[None], proj_part), "rep")


def solution(mesh):
    n_tab, n_rep = mesh.shape["tab"], mesh.shape["rep"]
    placed = (
        P("rep", "tab", None, None),
        P("rep", "tab", None, None),
        P(),
        P("rep", None, "tab", None),
        P("rep", None, "tab"),
        P(),
    )

    def body(*args):
        if n_rep % 2 == 0 and ROWS % (16 * n_rep) == 0 and args[2].shape[1] % (32 * n_rep) == 0:
            return fused(n_tab, n_rep, *args)
        return general(*args)

    return jax.shard_map(
        body,
        mesh=mesh,
        in_specs=placed,
        out_specs=(P("tab", None, None), P("tab", None, None)),
        check_vma=False,
    )
```

```python
import functools

import jax
import jax.numpy as jnp
from jax import lax
from jax.experimental import pallas as pl
from jax.experimental.pallas import tpu as pltpu
from jax.sharding import PartitionSpec as P

ROWS = 512
MESH = pl.DeviceIdType.MESH
BF16 = jnp.bfloat16
F32 = jnp.float32


SCALE_ROWS = 16


def encode(total):
    peak = jnp.maximum(jnp.max(jnp.abs(total), axis=0, keepdims=True), 1e-30)
    power = jnp.floor(jnp.log2(peak) + 1.01) - 15.0
    coded = jnp.floor(total * jnp.exp2(-power) + 0.5)
    coded = jnp.clip(coded, -32767.0, 32767.0).astype(jnp.int32).astype(jnp.int16)
    powers = jnp.broadcast_to(power, (SCALE_ROWS, total.shape[1]))
    return coded, powers.astype(jnp.int32).astype(jnp.int16)


def decode(coded, powers):
    scale = jnp.exp2(powers.astype(jnp.int32).astype(F32)[:1])
    return coded.astype(jnp.int32).astype(F32) * scale


def kernel(
    n_tab,
    n_rep,
    dproj_hbm,
    pooled_hbm,
    rows_hbm,
    lens_hbm,
    weight_hbm,
    dims_hbm,
    out_emb,
    out_proj,
    row_sum,
    proj_sum,
    emb_buf,
    live_weight,
    dproj_raw,
    pooled_raw,
    dproj_ref,
    pooled_ref,
    rows_ref,
    lens_ref,
    weight_ref,
    dims_ref,
    dproj_all,
    pooled_all,
    counts,
    row_own,
    row_wire,
    proj_own,
    proj_wire,
    load_sem,
    store_sem,
    own_sem,
    a_send,
    a_recv,
    y_send,
    y_recv,
    z_send,
    z_recv,
    g_send,
    g_recv,
):
    tab = lax.axis_index("tab")
    rep = lax.axis_index("rep")
    n_z = n_rep // 2
    y = lax.rem(rep, 2)
    z = rep // 2
    partner = rep + 1 - 2 * y
    n_samples, width = dproj_ref.shape[2], dproj_ref.shape[3]
    piece = pooled_ref.shape[1] // 2

    loads = [
        pltpu.make_async_copy(src, dst, load_sem.at[i])
        for i, (src, dst) in enumerate((
            (dproj_hbm, dproj_raw),
            (pooled_hbm, pooled_raw),
            (rows_hbm, rows_ref),
            (lens_hbm, lens_ref),
            (weight_hbm.at[tab], weight_ref),
            (dims_hbm, dims_ref),
        ))
    ]
    for copy in loads:
        copy.start()

    def remote(src, dst, send, recv, tab_to, rep_to):
        return pltpu.make_async_remote_copy(
            src_ref=src,
            dst_ref=dst,
            send_sem=send,
            recv_sem=recv,
            device_id=(tab_to, rep_to),
            device_id_type=MESH,
        )

    barrier = pltpu.get_barrier_semaphore()
    for k in range(1, n_tab):
        pl.semaphore_signal(
            barrier, inc=1, device_id=(lax.rem(tab + k, n_tab), rep), device_id_type=MESH
        )
    for k in range(1, n_z):
        pl.semaphore_signal(
            barrier, inc=1, device_id=(tab, lax.rem(rep + 2 * k, n_rep)), device_id_type=MESH
        )
    pl.semaphore_signal(barrier, inc=1, device_id=(tab, partner), device_id_type=MESH)
    loads[0].wait()
    by_table = jnp.transpose(dproj_raw[...], (1, 0, 2))
    for half in range(2):
        dproj_ref[half] = by_table[:, :, half * width : (half + 1) * width]
    pl.semaphore_wait(barrier, n_tab - 1 + n_z)

    def columns(first, second, which, at):
        if which < 2:
            return first.at[which, at]
        return second.at[at, pl.ds((which - 2) * piece, piece)]

    gathers = []
    for which in range(4):
        if which == 2:
            loads[1].wait()
            by_table = jnp.transpose(pooled_raw[...], (1, 0, 2))
        if which >= 2:
            at = (which - 2) * piece
            for table in range(n_tab):
                pooled_ref[table, at : at + piece] = by_table[table, :, at : at + piece].T
        copies = []
        for k in range(1, n_tab):
            to = lax.rem(tab + k, n_tab)
            copy = remote(
                columns(dproj_ref, pooled_ref, which, to),
                columns(dproj_all, pooled_all, which, tab),
                a_send.at[which, k], a_recv.at[which, k], to, rep,
            )
            copy.start()
            copies.append(copy)
        gathers.append(copies)
    own = [
        pltpu.make_async_copy(
            dproj_ref.at[half, tab], dproj_all.at[half, tab], own_sem.at[half]
        )
        for half in range(2)
    ]
    for copy in own:
        copy.start()

    for copy in loads[2:4]:
        copy.wait()
    named = rows_ref[...]
    slots = lax.broadcasted_iota(jnp.int32, named.shape, 0)
    named = jnp.where(slots < lens_ref[...], named, -1)
    step = 64

    def count(i, carry):
        at = pl.multiple_of(i * step, step)
        ids = lax.broadcasted_iota(jnp.int32, (step, named.shape[1]), 0) + at
        total = jnp.zeros((step, named.shape[1]), F32)
        for slot in range(named.shape[0]):
            total = total + jnp.where(named[slot : slot + 1, :] == ids, 1.0, 0.0)
        counts[pl.ds(at, step), :] = total.astype(BF16)
        return carry

    lax.fori_loop(0, counts.shape[0] // step, count, 0)

    buffers = [(row_own.at[i], row_wire.at[i], row_sum.at[i]) for i in range(2)]
    buffers += [(proj_own.at[i], proj_wire.at[i], proj_sum.at[i]) for i in range(2)]

    def send_pair(which):
        sums, wire, _ = buffers[which]
        wire[0] = sums[1 - y].astype(BF16)
        copy = remote(wire.at[0], wire.at[1], y_send.at[which], y_recv.at[which], tab, partner)
        copy.start()
        return copy

    def send_line(which, pair):
        sums, wire, _ = buffers[which]
        pair.wait_recv()
        total = sums[y] + wire[1].astype(F32)
        wire[2] = total.astype(BF16)
        copies = []
        for k in range(1, n_z):
            to = lax.rem(z + k, n_z)
            copy = remote(
                wire.at[2, to], wire.at[3, k], z_send.at[which, k], z_recv.at[which, k],
                tab, 2 * to + y,
            )
            copy.start()
            copies.append(copy)
        sums[y] = total
        return copies

    def send_sums(which, line):
        sums, wire, out = buffers[which]
        for copy in line:
            copy.wait_recv()
        total = sums[y, z]
        for k in range(1, n_z):
            total = total + wire[3, k].astype(F32)
        if which < 2:
            part = total.shape[0]
            coded, powers = encode(total)
            out[y, z, :part] = coded
            out[y, z, part:] = powers
        else:
            first = (which - 2) * piece + (y * n_z + z) * total.shape[0]
            at = lax.broadcasted_iota(jnp.int32, total.shape, 0) + first
            out[y, z] = jnp.where(at < limit, total, 0.0).astype(BF16)
        block = out.at[y, z]
        copies = []
        for k in range(1, n_z):
            copy = remote(
                block, block, g_send.at[which, 0, k], g_recv.at[which, 0, k],
                tab, 2 * lax.rem(z + k, n_z) + y,
            )
            copy.start()
            copies.append(copy)
        copy = remote(
            block, block, g_send.at[which, 1, 0], g_recv.at[which, 1, 0], tab, partner
        )
        copy.start()
        return copies, copy

    def forward(which, arriving):
        out = buffers[which][2]
        copies = []
        for k in range(1, n_z):
            arriving[k - 1].wait_recv()
            block = out.at[y, lax.rem(z - k + n_z, n_z)]
            copy = remote(
                block, block, g_send.at[which, 1, k], g_recv.at[which, 1, k], tab, partner
            )
            copy.start()
            copies.append(copy)
        return copies

    def project(half):
        total = None
        for k in range(n_tab):
            if k > 0:
                gathers[2 + half][k - 1].wait_recv()
            at = lax.rem(tab - k + n_tab, n_tab)
            block = (pooled_all if k > 0 else pooled_ref)[at, half * piece : (half + 1) * piece]
            both = jnp.concatenate([dproj_all[0, at], dproj_all[1, at]], axis=1)
            term = jnp.dot(block, both, preferred_element_type=F32)
            total = term if total is None else total + term
        proj_own[half] = total.reshape(proj_own.shape[1:])
        return send_pair(2 + half)

    for copy in loads[4:]:
        copy.wait()
    limit = weight_ref.shape[0] // 16 * dims_ref[tab]
    at_row = lax.broadcasted_iota(jnp.int32, weight_ref.shape, 0)
    live_weight[...] = jnp.where(at_row < limit, weight_ref[...].astype(F32), 0.0).astype(BF16)
    stores = [
        pltpu.make_async_copy(src, dst, store_sem.at[i])
        for i, (src, dst) in enumerate((
            (emb_buf.at[0], out_emb.at[y]),
            (emb_buf.at[1], out_emb.at[1 - y]),
            (proj_sum.at[0], out_proj.at[0]),
            (proj_sum.at[1], out_proj.at[1]),
        ))
    ]

    def table_rows(slot, half):
        part = row_sum.shape[3] - SCALE_ROWS
        total = jnp.concatenate(
            [
                jnp.concatenate(
                    [
                        decode(row_sum[i, half, at, :part], row_sum[i, half, at, part:])
                        for at in range(n_z)
                    ],
                    axis=0,
                )
                for i in range(2)
            ],
            axis=1,
        )
        high = total.astype(BF16)
        low = (total - high.astype(F32)).astype(BF16)
        weight = live_weight[...]
        emb_buf[slot] = lax.dot_general(
            high, weight, (((1,), (1,)), ((), ())), preferred_element_type=F32
        ) + lax.dot_general(low, weight, (((1,), (1,)), ((), ())), preferred_element_type=F32)
        stores[slot].start()

    pairs = []
    for half in range(2):
        own[half].wait()
        for copy in gathers[half]:
            copy.wait_recv()
        d_all = dproj_all[half].reshape(n_tab * n_samples, width)
        row_part = jnp.dot(counts[...], d_all, preferred_element_type=F32)
        row_own[half] = row_part.reshape(row_own.shape[1:])
        pairs.append(send_pair(half))
    line0 = send_line(0, pairs[0])
    line1 = send_line(1, pairs[1])
    pairs.append(project(0))
    sums0, last0 = send_sums(0, line0)
    pairs.append(project(1))
    sums1, last1 = send_sums(1, line1)
    line2 = send_line(2, pairs[2])
    line3 = send_line(3, pairs[3])
    sums2, last2 = send_sums(2, line2)
    fwd0 = forward(0, sums0)
    fwd1 = forward(1, sums1)
    table_rows(0, y)
    sums3, last3 = send_sums(3, line3)
    fwd2 = forward(2, sums2)
    for copy in [last0, last1, *fwd0, *fwd1]:
        copy.wait_recv()
    table_rows(1, 1 - y)
    fwd3 = forward(3, sums3)
    for half, copies in enumerate(([last2, *fwd2], [last3, *fwd3])):
        for copy in copies:
            copy.wait_recv()
        stores[2 + half].start()
    for copies in [*gathers, pairs, line0, line1, line2, line3, sums0, sums1, sums2, sums3]:
        for copy in copies:
            copy.wait_send()
    for copies in [[last0, last1, last2, last3], fwd0, fwd1, fwd2, fwd3]:
        for copy in copies:
            copy.wait_send()
    for copy in stores:
        copy.wait()


def finish(
    emb_from, proj_from, emb_to, proj_to, emb_buf, proj_in, proj_out, load_sem, store_sem
):
    tiles = emb_from.shape[0]
    loads = [pltpu.make_async_copy(proj_from, proj_in, load_sem.at[tiles])]
    stores = [pltpu.make_async_copy(proj_out, proj_to, store_sem.at[tiles])]
    for i in range(tiles):
        loads.append(pltpu.make_async_copy(emb_from.at[i], emb_buf.at[i], load_sem.at[i]))
        stores.append(pltpu.make_async_copy(emb_buf.at[i], emb_to.at[i], store_sem.at[i]))
    for copy in loads:
        copy.start()
    for i in range(tiles + 1):
        loads[i].wait()
        if i == 0:
            proj_out[...] = proj_in[...].astype(F32)
        stores[i].start()
    for copy in stores:
        copy.wait()


def fused(n_tab, n_rep, d_proj, pooled, proj, bag_rows, bag_lengths, dim_blocks):
    n_samples, width, widest = d_proj.shape[1], d_proj.shape[3], pooled.shape[3]
    group, bag = bag_rows.shape[1], bag_rows.shape[3]
    n_z = n_rep // 2
    part, proj_part = ROWS // n_rep, widest // 2 // n_rep
    hbm = pl.BlockSpec(memory_space=pltpu.HBM)
    dma = pltpu.SemaphoreType.DMA
    emb, proj_grad = pl.pallas_call(
        functools.partial(kernel, n_tab, n_rep),
        out_shape=(
            jax.ShapeDtypeStruct((2, ROWS // 2, widest), F32),
            jax.ShapeDtypeStruct((2, 2, n_z, proj_part, width), BF16),
        ),
        in_specs=[hbm] * 6,
        out_specs=(hbm, hbm),
        scratch_shapes=[
            pltpu.VMEM((2, 2, n_z, part + SCALE_ROWS, width // 2), jnp.int16),
            pltpu.VMEM((2, 2, n_z, proj_part, width), BF16),
            pltpu.VMEM((2, ROWS // 2, widest), F32),
            pltpu.VMEM((widest, width), BF16),
            pltpu.VMEM((n_samples, n_tab, width), BF16),
            pltpu.VMEM((n_samples, n_tab, widest), BF16),
            pltpu.VMEM((2, n_tab, n_samples, width // 2), BF16),
            pltpu.VMEM((n_tab, widest, n_samples), BF16),
            pltpu.VMEM((bag, group), jnp.int32),
            pltpu.VMEM((1, group), jnp.int32),
            pltpu.VMEM((widest, width), BF16),
            pltpu.SMEM((n_tab,), jnp.int32),
            pltpu.VMEM((2, n_tab, n_samples, width // 2), BF16),
            pltpu.VMEM((n_tab, widest, n_samples), BF16),
            pltpu.VMEM((ROWS, group), BF16),
            pltpu.VMEM((2, 2, n_z, part, width // 2), F32),
            pltpu.VMEM((2, 4, n_z, part, width // 2), BF16),
            pltpu.VMEM((2, 2, n_z, proj_part, width), F32),
            pltpu.VMEM((2, 4, n_z, proj_part, width), BF16),
            dma((6,)),
            dma((4,)),
            dma((2,)),
            dma((4, n_tab)),
            dma((4, n_tab)),
            dma((4,)),
            dma((4,)),
            dma((4, n_z)),
            dma((4, n_z)),
            dma((4, 2, n_z)),
            dma((4, 2, n_z)),
        ],
        compiler_params=pltpu.CompilerParams(
            collective_id=0, has_side_effects=True, vmem_limit_bytes=60 << 20
        ),
    )(
        d_proj[0],
        pooled[0],
        jnp.transpose(bag_rows[0, :, 0, :]),
        bag_lengths.reshape(1, group),
        proj,
        dim_blocks,
    )
    tiles = 4
    emb = emb.reshape(tiles, ROWS // tiles, widest)
    proj_grad = proj_grad.reshape(widest, width)
    emb, proj_grad = pl.pallas_call(
        finish,
        out_shape=(
            jax.ShapeDtypeStruct(emb.shape, F32),
            jax.ShapeDtypeStruct(proj_grad.shape, F32),
        ),
        in_specs=[hbm] * 2,
        out_specs=(hbm, hbm),
        scratch_shapes=[
            pltpu.VMEM(emb.shape, F32),
            pltpu.VMEM(proj_grad.shape, BF16),
            pltpu.VMEM(proj_grad.shape, F32),
            dma((tiles + 1,)),
            dma((tiles + 1,)),
        ],
        compiler_params=pltpu.CompilerParams(vmem_limit_bytes=60 << 20),
        cost_estimate=pl.CostEstimate(
            flops=0, bytes_accessed=8 * (ROWS + width) * widest, transcendentals=0
        ),
    )(emb, proj_grad)
    return emb.reshape(1, ROWS, widest), proj_grad.reshape(1, widest, width)


def general(d_proj, pooled, proj, bag_rows, bag_lengths, dim_blocks):
    widest = proj.shape[1]
    group_rows = bag_rows.shape[1]
    bag_size = bag_rows.shape[3]
    columns = jnp.arange(widest, dtype=jnp.int32)
    live = (columns[None, :] < (widest // 16 * dim_blocks)[:, None]).astype(F32)
    samples_proj = d_proj[0]
    masked_pool = jnp.where(live[None, :, :] > 0, pooled[0], jnp.zeros_like(pooled[0]))
    proj_part = lax.psum_scatter(
        jnp.einsum("bte,btp->tep", masked_pool, samples_proj, preferred_element_type=F32),
        "tab",
        scatter_dimension=0,
        tiled=True,
    )
    back = jnp.einsum("btp,tep->bte", samples_proj, proj, preferred_element_type=F32)
    back = (back * live[None, :, :]).astype(BF16)
    d_pooled = lax.all_to_all(back, "tab", split_axis=1, concat_axis=0, tiled=True)
    row_ids = jnp.arange(ROWS, dtype=jnp.int32)
    counts = jnp.zeros((group_rows, ROWS), F32)
    for slot in range(bag_size):
        hit = (bag_rows[0, :, 0, slot][:, None] == row_ids[None, :]) & (
            slot < bag_lengths[0, :, 0]
        )[:, None]
        counts = counts + hit.astype(F32)
    emb_part = lax.dot_general(
        counts.astype(BF16), d_pooled[:, 0, :], (((0,), (0,)), ((), ())),
        preferred_element_type=F32,
    )
    return lax.psum((emb_part[None], proj_part), "rep")


def solution(mesh):
    n_tab, n_rep = mesh.shape["tab"], mesh.shape["rep"]
    placed = (
        P("rep", "tab", None, None),
        P("rep", "tab", None, None),
        P(),
        P("rep", None, "tab", None),
        P("rep", None, "tab"),
        P(),
    )

    def body(*args):
        if n_rep % 2 == 0 and ROWS % (16 * n_rep) == 0 and args[2].shape[1] % (32 * n_rep) == 0:
            return fused(n_tab, n_rep, *args)
        return general(*args)

    return jax.shard_map(
        body,
        mesh=mesh,
        in_specs=placed,
        out_specs=(P("tab", None, None), P("tab", None, None)),
        check_vma=False,
    )
```

```python
import functools

import jax
import jax.numpy as jnp
from jax import lax
from jax.experimental import pallas as pl
from jax.experimental.pallas import tpu as pltpu
from jax.sharding import PartitionSpec as P

ROWS = 512
MESH = pl.DeviceIdType.MESH
BF16 = jnp.bfloat16
F32 = jnp.float32


SCALE_ROWS = 16


def encode(total):
    peak = jnp.maximum(jnp.max(jnp.abs(total), axis=0, keepdims=True), 1e-30)
    power = jnp.floor(jnp.log2(peak) + 1.01) - 15.0
    coded = jnp.floor(total * jnp.exp2(-power) + 0.5)
    coded = jnp.clip(coded, -32767.0, 32767.0).astype(jnp.int32).astype(jnp.int16)
    powers = jnp.broadcast_to(power, (SCALE_ROWS, total.shape[1]))
    return coded, powers.astype(jnp.int32).astype(jnp.int16)


def decode(coded, powers):
    scale = jnp.exp2(powers.astype(jnp.int32).astype(F32)[:1])
    return coded.astype(jnp.int32).astype(F32) * scale


def kernel(
    n_tab,
    n_rep,
    dproj_hbm,
    pooled_hbm,
    rows_hbm,
    lens_hbm,
    weight_hbm,
    dims_hbm,
    out_emb,
    out_proj,
    row_sum,
    proj_sum,
    emb_buf,
    live_weight,
    dproj_raw,
    pooled_raw,
    dproj_ref,
    pooled_ref,
    rows_ref,
    lens_ref,
    weight_ref,
    dims_ref,
    dproj_all,
    pooled_all,
    counts,
    row_own,
    row_wire,
    proj_own,
    proj_wire,
    load_sem,
    store_sem,
    own_sem,
    a_send,
    a_recv,
    y_send,
    y_recv,
    z_send,
    z_recv,
    g_send,
    g_recv,
):
    tab = lax.axis_index("tab")
    rep = lax.axis_index("rep")
    n_z = n_rep // 2
    y = lax.rem(rep, 2)
    z = rep // 2
    partner = rep + 1 - 2 * y
    n_samples, width = dproj_ref.shape[1], dproj_ref.shape[2]

    loads = [
        pltpu.make_async_copy(src, dst, load_sem.at[i])
        for i, (src, dst) in enumerate((
            (dproj_hbm, dproj_raw),
            (pooled_hbm, pooled_raw),
            (rows_hbm, rows_ref),
            (lens_hbm, lens_ref),
            (weight_hbm.at[tab], weight_ref),
            (dims_hbm, dims_ref),
        ))
    ]
    for copy in loads:
        copy.start()

    def remote(src, dst, send, recv, tab_to, rep_to):
        return pltpu.make_async_remote_copy(
            src_ref=src,
            dst_ref=dst,
            send_sem=send,
            recv_sem=recv,
            device_id=(tab_to, rep_to),
            device_id_type=MESH,
        )

    barrier = pltpu.get_barrier_semaphore()
    for k in range(1, n_tab):
        pl.semaphore_signal(
            barrier, inc=1, device_id=(lax.rem(tab + k, n_tab), rep), device_id_type=MESH
        )
    for k in range(1, n_z):
        pl.semaphore_signal(
            barrier, inc=1, device_id=(tab, lax.rem(rep + 2 * k, n_rep)), device_id_type=MESH
        )
    pl.semaphore_signal(barrier, inc=1, device_id=(tab, partner), device_id_type=MESH)
    loads[0].wait()
    dproj_ref[...] = jnp.transpose(dproj_raw[...], (1, 0, 2))
    pl.semaphore_wait(barrier, n_tab - 1 + n_z)

    gathers = []
    for which in range(2):
        src, dst = (dproj_ref, dproj_all) if which == 0 else (pooled_ref, pooled_all)
        if which == 1:
            loads[1].wait()
            by_table = jnp.transpose(pooled_raw[...], (1, 0, 2))
            for table in range(n_tab):
                pooled_ref[table] = by_table[table].T
        copies = []
        for k in range(1, n_tab):
            to = lax.rem(tab + k, n_tab)
            copy = remote(
                src.at[to], dst.at[tab], a_send.at[which, k], a_recv.at[which, k], to, rep
            )
            copy.start()
            copies.append(copy)
        gathers.append(copies)
    own = pltpu.make_async_copy(dproj_ref.at[tab], dproj_all.at[tab], own_sem.at[0])
    own.start()

    for copy in loads[2:4]:
        copy.wait()
    named = rows_ref[...]
    slots = lax.broadcasted_iota(jnp.int32, named.shape, 0)
    named = jnp.where(slots < lens_ref[...], named, -1)
    step = 64

    def count(i, carry):
        at = pl.multiple_of(i * step, step)
        ids = lax.broadcasted_iota(jnp.int32, (step, named.shape[1]), 0) + at
        total = jnp.zeros((step, named.shape[1]), F32)
        for slot in range(named.shape[0]):
            total = total + jnp.where(named[slot : slot + 1, :] == ids, 1.0, 0.0)
        counts[pl.ds(at, step), :] = total.astype(BF16)
        return carry

    lax.fori_loop(0, counts.shape[0] // step, count, 0)

    buffers = [(row_own, row_wire, row_sum), (proj_own, proj_wire, proj_sum)]

    def send_pair(which):
        sums, wire, _ = buffers[which]
        wire[0] = sums[1 - y].astype(BF16)
        copy = remote(wire.at[0], wire.at[1], y_send.at[which], y_recv.at[which], tab, partner)
        copy.start()
        return copy

    def send_line(which, pair):
        sums, wire, _ = buffers[which]
        pair.wait_recv()
        total = sums[y] + wire[1].astype(F32)
        wire[2] = total.astype(BF16)
        copies = []
        for k in range(1, n_z):
            to = lax.rem(z + k, n_z)
            copy = remote(
                wire.at[2, to], wire.at[3, k], z_send.at[which, k], z_recv.at[which, k],
                tab, 2 * to + y,
            )
            copy.start()
            copies.append(copy)
        sums[y] = total
        return copies

    def send_sums(which, line):
        sums, wire, out = buffers[which]
        for copy in line:
            copy.wait_recv()
        total = sums[y, z]
        for k in range(1, n_z):
            total = total + wire[3, k].astype(F32)
        if which == 0:
            part = total.shape[0]
            coded, powers = encode(total)
            out[y, z, :part] = coded
            out[y, z, part:] = powers
        else:
            first = (y * n_z + z) * total.shape[0]
            at = lax.broadcasted_iota(jnp.int32, total.shape, 0) + first
            out[y, z] = jnp.where(at < limit, total, 0.0).astype(BF16)
        block = out.at[y, z]
        copies = []
        for k in range(1, n_z):
            copy = remote(
                block, block, g_send.at[which, 0, k], g_recv.at[which, 0, k],
                tab, 2 * lax.rem(z + k, n_z) + y,
            )
            copy.start()
            copies.append(copy)
        return copies

    def forward(which, arriving):
        for copy in arriving:
            copy.wait_recv()
        half = buffers[which][2].at[y]
        copy = remote(half, half, g_send.at[which, 1, 0], g_recv.at[which, 1, 0], tab, partner)
        copy.start()
        return copy

    def project():
        total = None
        for k in range(n_tab):
            if k > 0:
                gathers[1][k - 1].wait_recv()
            at = lax.rem(tab - k + n_tab, n_tab)
            block = (pooled_all if k > 0 else pooled_ref)[at]
            term = jnp.dot(block, dproj_all[at], preferred_element_type=F32)
            total = term if total is None else total + term
        proj_own[...] = total.reshape(proj_own.shape)
        return send_pair(1)

    for copy in loads[4:]:
        copy.wait()
    limit = weight_ref.shape[0] // 16 * dims_ref[tab]
    at_row = lax.broadcasted_iota(jnp.int32, weight_ref.shape, 0)
    live_weight[...] = jnp.where(at_row < limit, weight_ref[...].astype(F32), 0.0).astype(BF16)
    stores = [
        pltpu.make_async_copy(src, dst, store_sem.at[i])
        for i, (src, dst) in enumerate((
            (emb_buf.at[0], out_emb.at[y]),
            (emb_buf.at[1], out_emb.at[1 - y]),
            (proj_sum.at[y], out_proj.at[y]),
            (proj_sum.at[1 - y], out_proj.at[1 - y]),
        ))
    ]

    def table_rows(slot, half):
        part = row_sum.shape[2] - SCALE_ROWS
        total = jnp.concatenate(
            [decode(row_sum[half, i, :part], row_sum[half, i, part:]) for i in range(n_z)], axis=0
        )
        high = total.astype(BF16)
        low = (total - high.astype(F32)).astype(BF16)
        weight = live_weight[...]
        emb_buf[slot] = lax.dot_general(
            high, weight, (((1,), (1,)), ((), ())), preferred_element_type=F32
        ) + lax.dot_general(low, weight, (((1,), (1,)), ((), ())), preferred_element_type=F32)
        stores[slot].start()

    own.wait()
    for copy in gathers[0]:
        copy.wait_recv()
    d_all = dproj_all[...].reshape(n_tab * n_samples, width)
    row_own[...] = jnp.dot(counts[...], d_all, preferred_element_type=F32).reshape(row_own.shape)
    pair0 = send_pair(0)
    line0 = send_line(0, pair0)
    pair1 = project()
    sums0 = send_sums(0, line0)
    line1 = send_line(1, pair1)
    fwd0 = forward(0, sums0)
    table_rows(0, y)
    sums1 = send_sums(1, line1)
    fwd0.wait_recv()
    table_rows(1, 1 - y)
    fwd1 = forward(1, sums1)
    stores[2].start()
    fwd1.wait_recv()
    stores[3].start()
    for copy in [*gathers[0], *gathers[1], pair0, pair1, *line0, *line1, *sums0, *sums1, fwd0, fwd1]:
        copy.wait_send()
    for copy in stores:
        copy.wait()


def finish(
    emb_from, proj_from, emb_to, proj_to, emb_buf, proj_in, proj_out, load_sem, store_sem
):
    tiles = emb_from.shape[0]
    loads = [pltpu.make_async_copy(proj_from, proj_in, load_sem.at[tiles])]
    stores = [pltpu.make_async_copy(proj_out, proj_to, store_sem.at[tiles])]
    for i in range(tiles):
        loads.append(pltpu.make_async_copy(emb_from.at[i], emb_buf.at[i], load_sem.at[i]))
        stores.append(pltpu.make_async_copy(emb_buf.at[i], emb_to.at[i], store_sem.at[i]))
    for copy in loads:
        copy.start()
    for i in range(tiles + 1):
        loads[i].wait()
        if i == 0:
            proj_out[...] = proj_in[...].astype(F32)
        stores[i].start()
    for copy in stores:
        copy.wait()


def fused(n_tab, n_rep, d_proj, pooled, proj, bag_rows, bag_lengths, dim_blocks):
    n_samples, width, widest = d_proj.shape[1], d_proj.shape[3], pooled.shape[3]
    group, bag = bag_rows.shape[1], bag_rows.shape[3]
    n_z = n_rep // 2
    part, proj_part = ROWS // n_rep, widest // n_rep
    hbm = pl.BlockSpec(memory_space=pltpu.HBM)
    dma = pltpu.SemaphoreType.DMA
    emb, proj_grad = pl.pallas_call(
        functools.partial(kernel, n_tab, n_rep),
        out_shape=(
            jax.ShapeDtypeStruct((2, ROWS // 2, widest), F32),
            jax.ShapeDtypeStruct((2, n_z, proj_part, width), BF16),
        ),
        in_specs=[hbm] * 6,
        out_specs=(hbm, hbm),
        scratch_shapes=[
            pltpu.VMEM((2, n_z, part + SCALE_ROWS, width), jnp.int16),
            pltpu.VMEM((2, n_z, proj_part, width), BF16),
            pltpu.VMEM((2, ROWS // 2, widest), F32),
            pltpu.VMEM((widest, width), BF16),
            pltpu.VMEM((n_samples, n_tab, width), BF16),
            pltpu.VMEM((n_samples, n_tab, widest), BF16),
            pltpu.VMEM((n_tab, n_samples, width), BF16),
            pltpu.VMEM((n_tab, widest, n_samples), BF16),
            pltpu.VMEM((bag, group), jnp.int32),
            pltpu.VMEM((1, group), jnp.int32),
            pltpu.VMEM((widest, width), BF16),
            pltpu.SMEM((n_tab,), jnp.int32),
            pltpu.VMEM((n_tab, n_samples, width), BF16),
            pltpu.VMEM((n_tab, widest, n_samples), BF16),
            pltpu.VMEM((ROWS, group), BF16),
            pltpu.VMEM((2, n_z, part, width), F32),
            pltpu.VMEM((4, n_z, part, width), BF16),
            pltpu.VMEM((2, n_z, proj_part, width), F32),
            pltpu.VMEM((4, n_z, proj_part, width), BF16),
            dma((6,)),
            dma((4,)),
            dma((1,)),
            dma((2, n_tab)),
            dma((2, n_tab)),
            dma((2,)),
            dma((2,)),
            dma((2, n_z)),
            dma((2, n_z)),
            dma((2, 2, n_z)),
            dma((2, 2, n_z)),
        ],
        compiler_params=pltpu.CompilerParams(
            collective_id=0, has_side_effects=True, vmem_limit_bytes=60 << 20
        ),
    )(
        d_proj[0],
        pooled[0],
        jnp.transpose(bag_rows[0, :, 0, :]),
        bag_lengths.reshape(1, group),
        proj,
        dim_blocks,
    )
    tiles = 4
    emb = emb.reshape(tiles, ROWS // tiles, widest)
    proj_grad = proj_grad.reshape(widest, width)
    emb, proj_grad = pl.pallas_call(
        finish,
        out_shape=(
            jax.ShapeDtypeStruct(emb.shape, F32),
            jax.ShapeDtypeStruct(proj_grad.shape, F32),
        ),
        in_specs=[hbm] * 2,
        out_specs=(hbm, hbm),
        scratch_shapes=[
            pltpu.VMEM(emb.shape, F32),
            pltpu.VMEM(proj_grad.shape, BF16),
            pltpu.VMEM(proj_grad.shape, F32),
            dma((tiles + 1,)),
            dma((tiles + 1,)),
        ],
        compiler_params=pltpu.CompilerParams(vmem_limit_bytes=60 << 20),
        cost_estimate=pl.CostEstimate(
            flops=0, bytes_accessed=8 * (ROWS + width) * widest, transcendentals=0
        ),
    )(emb, proj_grad)
    return emb.reshape(1, ROWS, widest), proj_grad.reshape(1, widest, width)


def general(d_proj, pooled, proj, bag_rows, bag_lengths, dim_blocks):
    widest = proj.shape[1]
    group_rows = bag_rows.shape[1]
    bag_size = bag_rows.shape[3]
    columns = jnp.arange(widest, dtype=jnp.int32)
    live = (columns[None, :] < (widest // 16 * dim_blocks)[:, None]).astype(F32)
    samples_proj = d_proj[0]
    masked_pool = jnp.where(live[None, :, :] > 0, pooled[0], jnp.zeros_like(pooled[0]))
    proj_part = lax.psum_scatter(
        jnp.einsum("bte,btp->tep", masked_pool, samples_proj, preferred_element_type=F32),
        "tab",
        scatter_dimension=0,
        tiled=True,
    )
    back = jnp.einsum("btp,tep->bte", samples_proj, proj, preferred_element_type=F32)
    back = (back * live[None, :, :]).astype(BF16)
    d_pooled = lax.all_to_all(back, "tab", split_axis=1, concat_axis=0, tiled=True)
    row_ids = jnp.arange(ROWS, dtype=jnp.int32)
    counts = jnp.zeros((group_rows, ROWS), F32)
    for slot in range(bag_size):
        hit = (bag_rows[0, :, 0, slot][:, None] == row_ids[None, :]) & (
            slot < bag_lengths[0, :, 0]
        )[:, None]
        counts = counts + hit.astype(F32)
    emb_part = lax.dot_general(
        counts.astype(BF16), d_pooled[:, 0, :], (((0,), (0,)), ((), ())),
        preferred_element_type=F32,
    )
    return lax.psum((emb_part[None], proj_part), "rep")


def solution(mesh):
    n_tab, n_rep = mesh.shape["tab"], mesh.shape["rep"]
    placed = (
        P("rep", "tab", None, None),
        P("rep", "tab", None, None),
        P(),
        P("rep", None, "tab", None),
        P("rep", None, "tab"),
        P(),
    )

    def body(*args):
        if n_rep % 2 == 0 and ROWS % (16 * n_rep) == 0 and args[2].shape[1] % (16 * n_rep) == 0:
            return fused(n_tab, n_rep, *args)
        return general(*args)

    return jax.shard_map(
        body,
        mesh=mesh,
        in_specs=placed,
        out_specs=(P("tab", None, None), P("tab", None, None)),
        check_vma=False,
    )
```

```python
import functools

import jax
import jax.numpy as jnp
from jax import lax
from jax.experimental import pallas as pl
from jax.experimental.pallas import tpu as pltpu
from jax.sharding import PartitionSpec as P

ROWS = 512
MESH = pl.DeviceIdType.MESH
BF16 = jnp.bfloat16
F32 = jnp.float32


SCALE_ROWS = 16


def encode(total):
    peak = jnp.maximum(jnp.max(jnp.abs(total), axis=0, keepdims=True), 1e-30)
    power = jnp.floor(jnp.log2(peak) + 1.01) - 15.0
    coded = jnp.floor(total * jnp.exp2(-power) + 0.5)
    coded = jnp.clip(coded, -32767.0, 32767.0).astype(jnp.int32).astype(jnp.int16)
    powers = jnp.broadcast_to(power, (SCALE_ROWS, total.shape[1]))
    return coded, powers.astype(jnp.int32).astype(jnp.int16)


def decode(coded, powers):
    scale = jnp.exp2(powers.astype(jnp.int32).astype(F32)[:1])
    return coded.astype(jnp.int32).astype(F32) * scale


def kernel(
    n_tab,
    n_rep,
    dproj_hbm,
    pooled_hbm,
    rows_hbm,
    lens_hbm,
    weight_hbm,
    dims_hbm,
    out_emb,
    out_proj,
    row_sum,
    proj_sum,
    emb_buf,
    live_weight,
    dproj_raw,
    pooled_raw,
    dproj_ref,
    pooled_ref,
    rows_ref,
    lens_ref,
    weight_ref,
    dims_ref,
    dproj_all,
    pooled_all,
    counts,
    row_own,
    row_wire,
    proj_own,
    proj_wire,
    load_sem,
    store_sem,
    own_sem,
    a_send,
    a_recv,
    y_send,
    y_recv,
    z_send,
    z_recv,
    g_send,
    g_recv,
):
    tab = lax.axis_index("tab")
    rep = lax.axis_index("rep")
    n_z = n_rep // 2
    y = lax.rem(rep, 2)
    z = rep // 2
    partner = rep + 1 - 2 * y
    n_samples, width = dproj_ref.shape[1], dproj_ref.shape[2]
    piece = pooled_ref.shape[1] // 2

    loads = [
        pltpu.make_async_copy(src, dst, load_sem.at[i])
        for i, (src, dst) in enumerate((
            (dproj_hbm, dproj_raw),
            (pooled_hbm, pooled_raw),
            (rows_hbm, rows_ref),
            (lens_hbm, lens_ref),
            (weight_hbm.at[tab], weight_ref),
            (dims_hbm, dims_ref),
        ))
    ]
    for copy in loads:
        copy.start()

    n_x = n_tab // 2
    offsets = [(dx, dc) for dx in range(1, n_x) for dc in range(2)] + [(0, 1)]
    x, core = tab // 2, lax.rem(tab, 2)

    def owner(dx, dc):
        return 2 * lax.rem(x + dx + n_x, n_x) + lax.rem(core + dc, 2)

    def remote(src, dst, send, recv, tab_to, rep_to):
        return pltpu.make_async_remote_copy(
            src_ref=src,
            dst_ref=dst,
            send_sem=send,
            recv_sem=recv,
            device_id=(tab_to, rep_to),
            device_id_type=MESH,
        )

    barrier = pltpu.get_barrier_semaphore()
    for k in range(1, n_tab):
        pl.semaphore_signal(
            barrier, inc=1, device_id=(lax.rem(tab + k, n_tab), rep), device_id_type=MESH
        )
    for k in range(1, n_z):
        pl.semaphore_signal(
            barrier, inc=1, device_id=(tab, lax.rem(rep + 2 * k, n_rep)), device_id_type=MESH
        )
    pl.semaphore_signal(barrier, inc=1, device_id=(tab, partner), device_id_type=MESH)
    loads[0].wait()
    dproj_ref[...] = jnp.transpose(dproj_raw[...], (1, 0, 2))
    pl.semaphore_wait(barrier, n_tab - 1 + n_z)

    def columns(ref, at, which):
        return ref.at[at] if which == 0 else ref.at[at, pl.ds((which - 1) * piece, piece)]

    gathers = []
    for which in range(3):
        if which == 1:
            loads[1].wait()
            by_table = jnp.transpose(pooled_raw[...], (1, 0, 2))
        if which > 0:
            at = (which - 1) * piece
            for table in range(n_tab):
                pooled_ref[table, at : at + piece] = by_table[table, :, at : at + piece].T
        src, dst = (dproj_ref, dproj_all) if which == 0 else (pooled_ref, pooled_all)
        copies = []
        for k, offset in enumerate(offsets):
            to = owner(*offset)
            copy = remote(
                columns(src, to, which), columns(dst, tab, which),
                a_send.at[which, k], a_recv.at[which, k], to, rep,
            )
            copy.start()
            copies.append(copy)
        gathers.append(copies)
    own = pltpu.make_async_copy(dproj_ref.at[tab], dproj_all.at[tab], own_sem.at[0])
    own.start()

    for copy in loads[2:4]:
        copy.wait()
    named = rows_ref[...]
    slots = lax.broadcasted_iota(jnp.int32, named.shape, 0)
    named = jnp.where(slots < lens_ref[...], named, -1)
    step = 64

    def count(i, carry):
        at = pl.multiple_of(i * step, step)
        ids = lax.broadcasted_iota(jnp.int32, (step, named.shape[1]), 0) + at
        total = jnp.zeros((step, named.shape[1]), F32)
        for slot in range(named.shape[0]):
            total = total + jnp.where(named[slot : slot + 1, :] == ids, 1.0, 0.0)
        counts[pl.ds(at, step), :] = total.astype(BF16)
        return carry

    lax.fori_loop(0, counts.shape[0] // step, count, 0)

    buffers = [
        (row_own, row_wire, row_sum),
        (proj_own.at[0], proj_wire.at[0], proj_sum.at[0]),
        (proj_own.at[1], proj_wire.at[1], proj_sum.at[1]),
    ]

    def send_pair(which):
        sums, wire, _ = buffers[which]
        wire[0] = sums[1 - y].astype(BF16)
        copy = remote(wire.at[0], wire.at[1], y_send.at[which], y_recv.at[which], tab, partner)
        copy.start()
        return copy

    def send_line(which, pair):
        sums, wire, _ = buffers[which]
        pair.wait_recv()
        total = sums[y] + wire[1].astype(F32)
        wire[2] = total.astype(BF16)
        copies = []
        for k in range(1, n_z):
            to = lax.rem(z + k, n_z)
            copy = remote(
                wire.at[2, to], wire.at[3, k], z_send.at[which, k], z_recv.at[which, k],
                tab, 2 * to + y,
            )
            copy.start()
            copies.append(copy)
        sums[y] = total
        return copies

    def send_sums(which, line):
        sums, wire, out = buffers[which]
        for copy in line:
            copy.wait_recv()
        total = sums[y, z]
        for k in range(1, n_z):
            total = total + wire[3, k].astype(F32)
        if which == 0:
            part = total.shape[0]
            coded, powers = encode(total)
            out[y, z, :part] = coded
            out[y, z, part:] = powers
        else:
            first = (which - 1) * piece + (y * n_z + z) * total.shape[0]
            at = lax.broadcasted_iota(jnp.int32, total.shape, 0) + first
            out[y, z] = jnp.where(at < limit, total, 0.0).astype(BF16)
        block = out.at[y, z]
        copies = []
        for k in range(1, n_z):
            copy = remote(
                block, block, g_send.at[which, 0, k], g_recv.at[which, 0, k],
                tab, 2 * lax.rem(z + k, n_z) + y,
            )
            copy.start()
            copies.append(copy)
        copy = remote(
            block, block, g_send.at[which, 1, 0], g_recv.at[which, 1, 0], tab, partner
        )
        copy.start()
        return copies, copy

    def forward(which, arriving):
        out = buffers[which][2]
        copies = []
        for k in range(1, n_z):
            arriving[k - 1].wait_recv()
            block = out.at[y, lax.rem(z - k + n_z, n_z)]
            copy = remote(
                block, block, g_send.at[which, 1, k], g_recv.at[which, 1, k], tab, partner
            )
            copy.start()
            copies.append(copy)
        return copies

    def project(half):
        total = None
        for k in [None, *reversed(range(n_tab - 1))]:
            at = tab
            if k is not None:
                gathers[1 + half][k].wait_recv()
                at = owner(-offsets[k][0], offsets[k][1])
            block = (pooled_ref if k is None else pooled_all)[at, half * piece : (half + 1) * piece]
            term = jnp.dot(block, dproj_all[at], preferred_element_type=F32)
            total = term if total is None else total + term
        proj_own[half] = total.reshape(proj_own.shape[1:])
        return send_pair(1 + half)

    for copy in loads[4:]:
        copy.wait()
    limit = weight_ref.shape[0] // 16 * dims_ref[tab]
    at_row = lax.broadcasted_iota(jnp.int32, weight_ref.shape, 0)
    live_weight[...] = jnp.where(at_row < limit, weight_ref[...].astype(F32), 0.0).astype(BF16)
    stores = [
        pltpu.make_async_copy(src, dst, store_sem.at[i])
        for i, (src, dst) in enumerate((
            (emb_buf.at[0], out_emb.at[y]),
            (emb_buf.at[1], out_emb.at[1 - y]),
            (proj_sum.at[0], out_proj.at[0]),
            (proj_sum.at[1], out_proj.at[1]),
        ))
    ]

    def table_rows(slot, half):
        part = row_sum.shape[2] - SCALE_ROWS
        total = jnp.concatenate(
            [decode(row_sum[half, i, :part], row_sum[half, i, part:]) for i in range(n_z)], axis=0
        )
        high = total.astype(BF16)
        low = (total - high.astype(F32)).astype(BF16)
        weight = live_weight[...]
        emb_buf[slot] = lax.dot_general(
            high, weight, (((1,), (1,)), ((), ())), preferred_element_type=F32
        ) + lax.dot_general(low, weight, (((1,), (1,)), ((), ())), preferred_element_type=F32)
        stores[slot].start()

    own.wait()
    for copy in gathers[0]:
        copy.wait_recv()
    d_all = dproj_all[...].reshape(n_tab * n_samples, width)
    row_own[...] = jnp.dot(counts[...], d_all, preferred_element_type=F32).reshape(row_own.shape)
    pair0 = send_pair(0)
    pair1 = project(0)
    line0 = send_line(0, pair0)
    pair2 = project(1)
    line1 = send_line(1, pair1)
    line2 = send_line(2, pair2)
    sums0, last0 = send_sums(0, line0)
    sums1, last1 = send_sums(1, line1)
    sums2, last2 = send_sums(2, line2)
    fwd0 = forward(0, sums0)
    fwd1 = forward(1, sums1)
    fwd2 = forward(2, sums2)
    table_rows(0, y)
    for copy in [last0, *fwd0]:
        copy.wait_recv()
    table_rows(1, 1 - y)
    for half, copies in enumerate(([last1, *fwd1], [last2, *fwd2])):
        for copy in copies:
            copy.wait_recv()
        stores[2 + half].start()
    for copy in [
        *gathers[0], *gathers[1], *gathers[2], pair0, pair1, pair2,
        *line0, *line1, *line2, *sums0, *sums1, *sums2,
        last0, last1, last2, *fwd0, *fwd1, *fwd2,
    ]:
        copy.wait_send()
    for copy in stores:
        copy.wait()


def finish(
    emb_from, proj_from, emb_to, proj_to, emb_buf, proj_in, proj_out, load_sem, store_sem
):
    tiles = emb_from.shape[0]
    loads = [pltpu.make_async_copy(proj_from, proj_in, load_sem.at[tiles])]
    stores = [pltpu.make_async_copy(proj_out, proj_to, store_sem.at[tiles])]
    for i in range(tiles):
        loads.append(pltpu.make_async_copy(emb_from.at[i], emb_buf.at[i], load_sem.at[i]))
        stores.append(pltpu.make_async_copy(emb_buf.at[i], emb_to.at[i], store_sem.at[i]))
    for copy in loads:
        copy.start()
    for i in range(tiles + 1):
        loads[i].wait()
        if i == 0:
            proj_out[...] = proj_in[...].astype(F32)
        stores[i].start()
    for copy in stores:
        copy.wait()


def fused(n_tab, n_rep, d_proj, pooled, proj, bag_rows, bag_lengths, dim_blocks):
    n_samples, width, widest = d_proj.shape[1], d_proj.shape[3], pooled.shape[3]
    group, bag = bag_rows.shape[1], bag_rows.shape[3]
    n_z = n_rep // 2
    part, proj_part = ROWS // n_rep, widest // 2 // n_rep
    hbm = pl.BlockSpec(memory_space=pltpu.HBM)
    dma = pltpu.SemaphoreType.DMA
    emb, proj_grad = pl.pallas_call(
        functools.partial(kernel, n_tab, n_rep),
        out_shape=(
            jax.ShapeDtypeStruct((2, ROWS // 2, widest), F32),
            jax.ShapeDtypeStruct((2, 2, n_z, proj_part, width), BF16),
        ),
        in_specs=[hbm] * 6,
        out_specs=(hbm, hbm),
        scratch_shapes=[
            pltpu.VMEM((2, n_z, part + SCALE_ROWS, width), jnp.int16),
            pltpu.VMEM((2, 2, n_z, proj_part, width), BF16),
            pltpu.VMEM((2, ROWS // 2, widest), F32),
            pltpu.VMEM((widest, width), BF16),
            pltpu.VMEM((n_samples, n_tab, width), BF16),
            pltpu.VMEM((n_samples, n_tab, widest), BF16),
            pltpu.VMEM((n_tab, n_samples, width), BF16),
            pltpu.VMEM((n_tab, widest, n_samples), BF16),
            pltpu.VMEM((bag, group), jnp.int32),
            pltpu.VMEM((1, group), jnp.int32),
            pltpu.VMEM((widest, width), BF16),
            pltpu.SMEM((n_tab,), jnp.int32),
            pltpu.VMEM((n_tab, n_samples, width), BF16),
            pltpu.VMEM((n_tab, widest, n_samples), BF16),
            pltpu.VMEM((ROWS, group), BF16),
            pltpu.VMEM((2, n_z, part, width), F32),
            pltpu.VMEM((4, n_z, part, width), BF16),
            pltpu.VMEM((2, 2, n_z, proj_part, width), F32),
            pltpu.VMEM((2, 4, n_z, proj_part, width), BF16),
            dma((6,)),
            dma((4,)),
            dma((1,)),
            dma((3, n_tab)),
            dma((3, n_tab)),
            dma((3,)),
            dma((3,)),
            dma((3, n_z)),
            dma((3, n_z)),
            dma((3, 2, n_z)),
            dma((3, 2, n_z)),
        ],
        compiler_params=pltpu.CompilerParams(
            collective_id=0, has_side_effects=True, vmem_limit_bytes=60 << 20
        ),
    )(
        d_proj[0],
        pooled[0],
        jnp.transpose(bag_rows[0, :, 0, :]),
        bag_lengths.reshape(1, group),
        proj,
        dim_blocks,
    )
    tiles = 4
    emb = emb.reshape(tiles, ROWS // tiles, widest)
    proj_grad = proj_grad.reshape(widest, width)
    emb, proj_grad = pl.pallas_call(
        finish,
        out_shape=(
            jax.ShapeDtypeStruct(emb.shape, F32),
            jax.ShapeDtypeStruct(proj_grad.shape, F32),
        ),
        in_specs=[hbm] * 2,
        out_specs=(hbm, hbm),
        scratch_shapes=[
            pltpu.VMEM(emb.shape, F32),
            pltpu.VMEM(proj_grad.shape, BF16),
            pltpu.VMEM(proj_grad.shape, F32),
            dma((tiles + 1,)),
            dma((tiles + 1,)),
        ],
        compiler_params=pltpu.CompilerParams(vmem_limit_bytes=60 << 20),
        cost_estimate=pl.CostEstimate(
            flops=0, bytes_accessed=8 * (ROWS + width) * widest, transcendentals=0
        ),
    )(emb, proj_grad)
    return emb.reshape(1, ROWS, widest), proj_grad.reshape(1, widest, width)


def general(d_proj, pooled, proj, bag_rows, bag_lengths, dim_blocks):
    widest = proj.shape[1]
    group_rows = bag_rows.shape[1]
    bag_size = bag_rows.shape[3]
    columns = jnp.arange(widest, dtype=jnp.int32)
    live = (columns[None, :] < (widest // 16 * dim_blocks)[:, None]).astype(F32)
    samples_proj = d_proj[0]
    masked_pool = jnp.where(live[None, :, :] > 0, pooled[0], jnp.zeros_like(pooled[0]))
    proj_part = lax.psum_scatter(
        jnp.einsum("bte,btp->tep", masked_pool, samples_proj, preferred_element_type=F32),
        "tab",
        scatter_dimension=0,
        tiled=True,
    )
    back = jnp.einsum("btp,tep->bte", samples_proj, proj, preferred_element_type=F32)
    back = (back * live[None, :, :]).astype(BF16)
    d_pooled = lax.all_to_all(back, "tab", split_axis=1, concat_axis=0, tiled=True)
    row_ids = jnp.arange(ROWS, dtype=jnp.int32)
    counts = jnp.zeros((group_rows, ROWS), F32)
    for slot in range(bag_size):
        hit = (bag_rows[0, :, 0, slot][:, None] == row_ids[None, :]) & (
            slot < bag_lengths[0, :, 0]
        )[:, None]
        counts = counts + hit.astype(F32)
    emb_part = lax.dot_general(
        counts.astype(BF16), d_pooled[:, 0, :], (((0,), (0,)), ((), ())),
        preferred_element_type=F32,
    )
    return lax.psum((emb_part[None], proj_part), "rep")


def solution(mesh):
    n_tab, n_rep = mesh.shape["tab"], mesh.shape["rep"]
    placed = (
        P("rep", "tab", None, None),
        P("rep", "tab", None, None),
        P(),
        P("rep", None, "tab", None),
        P("rep", None, "tab"),
        P(),
    )

    def body(*args):
        if n_rep % 2 == 0 and ROWS % (16 * n_rep) == 0 and args[2].shape[1] % (32 * n_rep) == 0:
            return fused(n_tab, n_rep, *args)
        return general(*args)

    return jax.shard_map(
        body,
        mesh=mesh,
        in_specs=placed,
        out_specs=(P("tab", None, None), P("tab", None, None)),
        check_vma=False,
    )
```
